32 devices in a mesh: cfg: 2 (over core), seq: 16 (over z, y, x).
Axes of the slice: x: 2, y: 2, z: 4, core: 2. Of those that a mesh axis runs over, the one named last changes fastest.
Arguments:
- queries: bfloat16 [2, 512, 2432], P('cfg', 'seq'), may hold values from -6 to 6
- image_keys: bfloat16 [2, 512, 2432], P('cfg', 'seq'), may hold values from -6 to 6
- image_values: bfloat16 [2, 512, 2432], P('cfg', 'seq'), may hold values from -6 to 6
- text_keys: bfloat16 [2, 64, 2432], P('cfg', 'seq'), may hold values from -6 to 6
- text_values: bfloat16 [2, 64, 2432], P('cfg', 'seq'), may hold values from -6 to 6
- hidden_in: bfloat16 [2, 512, 2432], P('cfg', 'seq'), may hold values from -6 to 6
- modulation: float32 [2, 6, 2432], P('cfg'), may hold values from 0.25 to 1.75
- w_out: bfloat16 [2432, 2432], replicated, may hold values from -0.125 to 0.125
- w_up: bfloat16 [2432, 9728], P(None, 'seq'), may hold values from -0.125 to 0.125
- w_down: bfloat16 [9728, 2432], P('seq'), may hold values from -0.0625 to 0.0625
- w_final: bfloat16 [2432, 64], replicated, may hold values from -0.125 to 0.125
- latent: float32 [512, 64], P('seq', 'cfg'), may hold values from -6 to 6
- text_len: int32 [2], P('cfg'), may hold values from 8 to 64, as said below
- step_index: int32 [1], replicated, may hold values from 0 to 26
- guidance: float32 [1], replicated, may hold values from 3.5 to 7
Outputs:
- velocity: float32 [512, 64], P('seq', 'cfg')
- next_latent: float32 [512, 64], P('seq', 'cfg')
The draws below stay inside these ranges and needn't reach their ends.
Inputs may be any that keep to these rules, and one draw needn't show every extreme that they name: `text_len`: in every draw one of the two halves has exactly 64 valid text tokens.
All inputs are finite; a program needn't handle non-finite values.
Results may differ from the reference program's by a relative error of at most 0.0095.
Values may be sent and summed in bfloat16 or wider, within the bound.
A program may use at most 128 MiB of HBM per device.

```python
import jax
import jax.numpy as jnp
from jax import lax

D = 2432
HEADS = 38
HEAD_DIM = 64
FF = 9728
OUT_CH = 64
STEPS = 28
IMG = 512
TXT = 64
TXT_MAX = 64


def shared_direction(key):
    spread = (2.0 / HEAD_DIM ** 0.5) ** 0.5
    return spread * jax.random.normal(jax.random.fold_in(key, 31), (2, 1, D), jnp.float32)


def drawn_pair(key):
    common = shared_direction(key)
    query_draw = jnp.clip(1.3 * jax.random.normal(jax.random.fold_in(key, 11), (2, IMG, D), jnp.float32) + common, -6.0, 6.0)
    key_draw = jnp.clip(1.3 * jax.random.normal(jax.random.fold_in(key, 12), (2, IMG, D), jnp.float32), -6.0, 6.0)
    return (query_draw, key_draw)


def draw_queries(key, part):
    return drawn_pair(key)[0].astype(jnp.bfloat16)


def draw_image_keys(key, part):
    return drawn_pair(key)[1].astype(jnp.bfloat16)


def draw_text_keys(key, part):
    common = shared_direction(key)
    noise = 1.3 * jax.random.normal(jax.random.fold_in(key, 41), (2, TXT, D), jnp.float32)
    return jnp.clip(noise + common, -6.0, 6.0).astype(jnp.bfloat16)


def draw_image_values(key, part):
    centre = 0.8 * jax.random.normal(jax.random.fold_in(key, 51), (2, 1, D), jnp.float32)
    noise = 0.8 * jax.random.normal(jax.random.fold_in(key, 52), (2, IMG, D), jnp.float32)
    return jnp.clip(centre + noise, -6.0, 6.0).astype(jnp.bfloat16)


def draw_text_values(key, part):
    centre = 0.8 * jax.random.normal(jax.random.fold_in(key, 61), (2, 1, D), jnp.float32)
    noise = 0.8 * jax.random.normal(jax.random.fold_in(key, 62), (2, TXT, D), jnp.float32)
    return jnp.clip(centre + noise, -6.0, 6.0).astype(jnp.bfloat16)


def draw_w_down(key, part):
    deviation = FF ** (-0.5)
    column_signs = jnp.where(jax.random.bernoulli(jax.random.fold_in(key, 71), 0.5, (1, D)), 1.0, -1.0)
    noise = jnp.clip(deviation * jax.random.normal(jax.random.fold_in(key, 73), (FF, D), jnp.float32), -6.0 * deviation, 6.0 * deviation)
    common = 0.0002 * column_signs
    return jnp.clip(noise + common, -0.0625, 0.0625).astype(jnp.bfloat16)


def draw_text_len(key, part):
    which = jax.random.randint(jax.random.fold_in(key, 21), (), 0, 2)
    other = jax.random.randint(jax.random.fold_in(key, 22), (), 8, TXT_MAX + 1)
    return jnp.where(jnp.arange(2) == which, TXT_MAX, other).astype(jnp.int32)


def block_levels(key, extent, pieces, low, top_value):
    gain, own = 1.0, jax.random.fold_in(key, 6)
    for position, parts in pieces:
        draws = jnp.exp(jax.random.uniform(jax.random.fold_in(own, position), (parts,), jnp.float32, low / len(pieces), top_value / len(pieces)))
        gain = gain * jnp.repeat(draws, extent[position] // parts).reshape([-1 if axis == position else 1 for axis in range(len(extent))])
    return gain


def gaussian(own_key, extent, scale, bound, cuts=(), kind=jnp.bfloat16):
    values = jax.random.normal(own_key, extent, jnp.float32) * scale
    if len(cuts) > 0:
        values = block_levels(own_key, extent, cuts, -0.22, 0.18) * values
    return jnp.clip(values, min=-bound, max=bound).astype(kind)


def setup_inputs(seed: int = 0) -> dict:
    streams_of = jax.random.split(jax.random.key(seed), 16)
    return {
        "queries": draw_queries(jax.random.fold_in(streams_of[15], 71), 0),
        "image_keys": draw_image_keys(jax.random.fold_in(streams_of[15], 71), 0),
        "image_values": draw_image_values(jax.random.fold_in(streams_of[15], 71), 0),
        "text_keys": draw_text_keys(jax.random.fold_in(streams_of[15], 71), 0),
        "text_values": draw_text_values(jax.random.fold_in(streams_of[15], 71), 0),
        "hidden_in": gaussian(streams_of[5], (2, IMG, D), 1.0, 6.0, ((0, 2), (1, 16))),
        "modulation": jnp.clip(0.25 + 1.5 * jax.random.uniform(streams_of[6], (2, 6, D), jnp.float32) ** block_levels(streams_of[6], (2, 6, D), ((0, 2),), -0.2, 0.2), 0.25, 1.75),
        "w_out": gaussian(streams_of[7], (D, D), D ** -0.5, 0.125),
        "w_up": gaussian(streams_of[8], (D, FF), D ** -0.5, 0.125, ((1, 16),)),
        "w_down": draw_w_down(jax.random.fold_in(streams_of[15], 71), 0),
        "w_final": gaussian(streams_of[10], (D, OUT_CH), D ** -0.5, 0.125),
        "latent": gaussian(streams_of[11], (IMG, OUT_CH), 1.0, 6.0, ((0, 16), (1, 2)), jnp.float32),
        "text_len": draw_text_len(jax.random.fold_in(streams_of[15], 71), 0),
        "step_index": jax.random.randint(streams_of[13], (1,), 0, STEPS - 1).astype(jnp.int32),
        "guidance": jnp.clip(jax.random.uniform(streams_of[14], (1,), jnp.float32, 3.5, 7.0), 3.5, 7.0),
    }


shift_value = 3.0
norm_eps = 1e-06

def layer_norm(values):
    centred = values - lax.optimization_barrier(jnp.mean(values, -1, keepdims=True))
    return centred / jnp.sqrt(lax.optimization_barrier(jnp.mean(centred * centred, -1, keepdims=True)) + norm_eps)

def sigma_at(index):
    frac = 1.0 - index.astype(jnp.float32) / STEPS
    return shift_value * frac / (1.0 + (shift_value - 1.0) * frac)

def half_velocity(query_half, key_rows, value_rows, key_valid, hidden_half, mods, w_out, w_up, w_down, w_final):
    score_scale = HEAD_DIM ** (-0.5)
    count = key_rows.shape[0]
    q_heads = query_half.reshape(IMG, HEADS, HEAD_DIM).transpose(1, 0, 2)
    k_heads = key_rows.reshape(count, HEADS, HEAD_DIM).transpose(1, 0, 2)
    v_heads = value_rows.reshape(count, HEADS, HEAD_DIM).transpose(1, 0, 2)

    def one_head(triple):
        q_one, k_one, v_one = triple
        scores = jnp.dot(q_one, k_one.T, preferred_element_type=jnp.float32) * score_scale
        scores = jnp.where(key_valid[None, :], scores, -1e+30)
        row_top = lax.optimization_barrier(jnp.max(scores, -1, keepdims=True))
        weights = jnp.exp(scores - row_top)
        total = lax.optimization_barrier(jnp.sum(weights, -1, keepdims=True))
        return jnp.dot(weights.astype(jnp.bfloat16), v_one, preferred_element_type=jnp.float32) / total
    per_head = lax.map(one_head, (q_heads, k_heads, v_heads))
    attended = per_head.transpose(1, 0, 2).reshape(IMG, D).astype(jnp.bfloat16)
    projected = jnp.dot(attended, w_out, preferred_element_type=jnp.float32)
    middle = hidden_half.astype(jnp.float32) + mods[0] * projected
    normed = (layer_norm(middle) * (1.0 + mods[2]) + mods[1]).astype(jnp.bfloat16)
    hidden = jax.nn.gelu(jnp.dot(normed, w_up, preferred_element_type=jnp.float32), approximate=True).astype(jnp.bfloat16)
    mlp_out = jnp.dot(hidden, w_down, preferred_element_type=jnp.float32)
    final = middle + mods[3] * mlp_out
    head_in = (layer_norm(final) * (1.0 + mods[5]) + mods[4]).astype(jnp.bfloat16)
    return jnp.dot(head_in, w_final, preferred_element_type=jnp.float32)

def reference(queries, image_keys, image_values, text_keys, text_values, hidden_in, modulation, w_out, w_up, w_down, w_final, latent, text_len, step_index, guidance):
    results = []
    for branch in range(2):
        key_rows = jnp.concatenate([image_keys[branch], text_keys[branch]], 0)
        value_rows = jnp.concatenate([image_values[branch], text_values[branch]], 0)
        slots = jnp.arange(TXT, dtype=jnp.int32)
        key_valid = jnp.concatenate([jnp.ones((IMG,), bool), slots < text_len[branch]], 0)
        results.append(half_velocity(queries[branch], key_rows, value_rows, key_valid, hidden_in[branch], modulation[branch], w_out, w_up, w_down, w_final))
    cond_part, uncond_part = results
    velocity = uncond_part + guidance[0] * (cond_part - uncond_part)
    step_size = sigma_at(step_index[0] + 1) - sigma_at(step_index[0])
    next_latent = latent + step_size * velocity
    return (velocity, next_latent)
```

```python
import functools

import jax
import jax.numpy as jnp
from jax import lax
from jax.experimental import pallas as pl
from jax.experimental.pallas import tpu as pltpu
from jax.sharding import PartitionSpec as P

HEADS = 38
HEAD_DIM = 64
STEPS = 28


shift_value = 3.0
norm_eps = 1e-06


def partner_2(value, axis, bit):
    mask = 2**bit
    pairs = [(source, source ^ mask) for source in range(lax.axis_size(axis))]
    return lax.ppermute(value, axis, pairs)


def layer_norm(values):
    centred = values - jnp.mean(values, -1, keepdims=True)
    return centred / jnp.sqrt(jnp.mean(centred * centred, -1, keepdims=True) + norm_eps)


def sigma_at(index):
    frac = 1.0 - index.astype(jnp.float32) / STEPS
    return shift_value * frac / (1.0 + (shift_value - 1.0) * frac)


def ffn_kernel(
    ca, norm_ref, up_ref, down_ref, out_ref, wu, wd, g, pf, pb, ry0, ry1, rx0, rx1, rxa, ryb, rz, s0, s1, s2,
    wsem, ssem, gsem, dsem, esem
):
    me = lax.axis_index("seq")
    mz = me // 4
    mx = lax.rem(me, 2)
    my = lax.rem(me // 2, 2)
    xn = mz * 4 + my * 2 + (1 - mx)
    yn = mz * 4 + (1 - my) * 2 + mx
    zs = [lax.rem(mz + k, 4) for k in range(4)]
    zn = [z * 4 + my * 2 + mx for z in zs]
    width = norm_ref.shape[1]
    cols = (pl.ds(0, ca), pl.ds(ca, width - ca))
    a, b = cols
    load_up = pltpu.make_async_copy(up_ref, wu, wsem.at[0])
    load_down = pltpu.make_async_copy(down_ref, wd, wsem.at[1])
    load_up.start()
    load_down.start()
    barrier = pltpu.get_barrier_semaphore()
    peers = (xn, yn, zn[1], zn[2], zn[3])
    for peer in peers:
        pl.semaphore_signal(barrier, inc=1, device_id={"seq": peer}, device_id_type=pl.DeviceIdType.MESH)
    sent = []

    def send(src, dst, recv, peer):
        copy = pltpu.make_async_remote_copy(
            src_ref=src, dst_ref=dst, send_sem=ssem.at[len(sent)], recv_sem=recv,
            device_id={"seq": peer}, device_id_type=pl.DeviceIdType.MESH,
        )
        copy.start()
        sent.append(copy)

    def arrived(dst, recv):
        pltpu.make_async_remote_copy(
            src_ref=dst, dst_ref=dst, send_sem=ssem.at[0], recv_sem=recv,
            device_id={"seq": xn}, device_id_type=pl.DeviceIdType.MESH,
        ).wait_recv()

    g[0, mz] = norm_ref[...]
    pl.semaphore_wait(barrier, len(peers))
    for k in (2, 1, 3):
        send(norm_ref, g.at[0, mz], gsem.at[0, mz], zn[k])
    send(norm_ref, g.at[1, mz], gsem.at[1, mz], xn)
    send(norm_ref, g.at[2, mz], gsem.at[2, mz], yn)
    for k in (1, 3, 2):
        z = zs[k]
        arrived(g.at[0, z], gsem.at[0, z])
        send(g.at[0, z], g.at[1, z], gsem.at[1, z], xn)
        send(g.at[0, z], g.at[2, z], gsem.at[2, z], yn)

    def up(q):
        rows = g[q].reshape(128, width)
        wide = jnp.dot(rows, wu[...], preferred_element_type=jnp.float32)
        return jax.nn.gelu(wide, approximate=True).astype(jnp.bfloat16)

    def down(hid, half):
        made = jnp.dot(hid, wd[:, cols[half]], preferred_element_type=jnp.float32)
        return made.reshape(4, 32, made.shape[1])

    load_up.wait()
    for k in (0, 1):
        z = zs[k]
        arrived(g.at[1, z], gsem.at[1, z])
        send(g.at[1, z, :, a], g.at[3, z, :, a], gsem.at[3, z], yn)
        arrived(g.at[2, z], gsem.at[2, z])
        send(g.at[2, z, :, b], g.at[3, z, :, b], gsem.at[4, z], xn)
    hid0 = up(0)
    for k in (3, 2):
        z = zs[k]
        arrived(g.at[1, z], gsem.at[1, z])
        send(g.at[1, z, :, a], g.at[3, z, :, a], gsem.at[3, z], yn)
        arrived(g.at[2, z], gsem.at[2, z])
        send(g.at[2, z, :, b], g.at[3, z, :, b], gsem.at[4, z], xn)
    load_down.wait()
    hid1 = up(1)
    pb[1, :, :, b] = down(hid1, 1).astype(jnp.bfloat16)
    send(pb.at[1, :, :, b], rx0, dsem.at[0], xn)
    hid2 = up(2)
    pb[2, :, :, a] = down(hid2, 0).astype(jnp.bfloat16)
    send(pb.at[2, :, :, a], ry0, dsem.at[1], yn)
    pf[1, :, :, a] = down(hid1, 0)
    pf[2, :, :, b] = down(hid2, 1)
    pf[0, :, :, a] = down(hid0, 0)
    pf[0, :, :, b] = down(hid0, 1)
    for z in zs:
        arrived(g.at[3, z, :, a], gsem.at[3, z])
        arrived(g.at[3, z, :, b], gsem.at[4, z])
    hid3 = up(3)
    order = (2, 1, 3, 0)
    pb[3, :, :, a] = down(hid3, 0).astype(jnp.bfloat16)
    for k in order:
        send(pb.at[3, zs[k], :, a], ry1.at[zs[k]], esem.at[0, zs[k]], yn)
    pb[3, :, :, b] = down(hid3, 1).astype(jnp.bfloat16)
    for k in order:
        send(pb.at[3, zs[k], :, b], rx1.at[zs[k]], esem.at[1, zs[k]], xn)
    for k in order:
        z = zs[k]
        arrived(ry1.at[z], esem.at[0, z])
        s1[z] = (pf[1, z, :, a] + ry1[z].astype(jnp.float32)).astype(jnp.bfloat16)
        send(s1.at[z], rxa.at[z], esem.at[2, z], xn)
        arrived(rx1.at[z], esem.at[1, z])
        s2[z] = (pf[2, z, :, b] + rx1[z].astype(jnp.float32)).astype(jnp.bfloat16)
        send(s2.at[z], ryb.at[z], esem.at[3, z], yn)
    arrived(rx0, dsem.at[0])
    arrived(ry0, dsem.at[1])
    for k in order:
        z = zs[k]
        arrived(rxa.at[z], esem.at[2, z])
        arrived(ryb.at[z], esem.at[3, z])
        sum_a = pf[0, z, :, a] + ry0[z].astype(jnp.float32) + rxa[z].astype(jnp.float32)
        sum_b = pf[0, z, :, b] + rx0[z].astype(jnp.float32) + ryb[z].astype(jnp.float32)
        if k:
            s0[z, :, a] = sum_a.astype(jnp.bfloat16)
            s0[z, :, b] = sum_b.astype(jnp.bfloat16)
            send(s0.at[z], rz.at[mz], esem.at[4, mz], zn[k])
        else:
            out_ref[:, a] = sum_a
            out_ref[:, b] = sum_b
    for k in (1, 3, 2):
        arrived(rz.at[zs[k]], esem.at[4, zs[k]])
        out_ref[...] += rz[zs[k]].astype(jnp.float32)
    for copy in sent:
        copy.wait_send()


def ffn_16(normed, w_up, w_down):
    rows, width = normed.shape
    hidden = w_up.shape[1]
    ca = (width // 128 + 1) // 2 * 128
    cb = width - ca
    half = jnp.bfloat16
    return pl.pallas_call(
        functools.partial(ffn_kernel, ca),
        out_shape=jax.ShapeDtypeStruct((rows, width), jnp.float32),
        in_specs=[
            pl.BlockSpec(memory_space=pltpu.VMEM),
            pl.BlockSpec(memory_space=pl.ANY),
            pl.BlockSpec(memory_space=pl.ANY),
        ],
        out_specs=pl.BlockSpec(memory_space=pltpu.VMEM),
        scratch_shapes=[
            pltpu.VMEM((width, hidden), half),
            pltpu.VMEM((hidden, width), half),
            pltpu.VMEM((4, 4, rows, width), half),
            pltpu.VMEM((3, 4, rows, width), jnp.float32),
            pltpu.VMEM((4, 4, rows, width), half),
            pltpu.VMEM((4, rows, ca), half),
            pltpu.VMEM((4, rows, ca), half),
            pltpu.VMEM((4, rows, cb), half),
            pltpu.VMEM((4, rows, cb), half),
            pltpu.VMEM((4, rows, ca), half),
            pltpu.VMEM((4, rows, cb), half),
            pltpu.VMEM((4, rows, width), half),
            pltpu.VMEM((4, rows, width), half),
            pltpu.VMEM((4, rows, ca), half),
            pltpu.VMEM((4, rows, cb), half),
            pltpu.SemaphoreType.DMA((2,)),
            pltpu.SemaphoreType.DMA((48,)),
            pltpu.SemaphoreType.DMA((5, 4)),
            pltpu.SemaphoreType.DMA((2,)),
            pltpu.SemaphoreType.DMA((5, 4)),
        ],
        cost_estimate=pl.CostEstimate(
            flops=4 * 16 * rows * width * hidden, bytes_accessed=4 * width * hidden, transcendentals=16 * rows * hidden
        ),
        compiler_params=pltpu.CompilerParams(
            collective_id=0, has_side_effects=True, vmem_limit_bytes=44 * 2**20
        ),
    )(normed, w_up, w_down)


def ffn_any(normed, w_up, w_down):
    hidden_all = jax.nn.gelu(
        jnp.dot(
            lax.all_gather(normed, "seq", axis=0, tiled=True),
            w_up,
            preferred_element_type=jnp.float32,
        ),
        approximate=True,
    ).astype(jnp.bfloat16)
    mlp_out = lax.psum_scatter(
        jnp.dot(hidden_all, w_down, preferred_element_type=jnp.float32),
        "seq",
        scatter_dimension=0,
        tiled=True,
    )
    return mlp_out


def body(
    queries,
    image_keys,
    image_values,
    text_keys,
    text_values,
    hidden_in,
    modulation,
    w_out,
    w_up,
    w_down,
    w_final,
    latent,
    text_len,
    step_index,
    guidance,
):
    img_rows = queries.shape[1]
    text_rows = text_keys.shape[1]
    both_rows = img_rows + text_rows
    width = queries.shape[2]
    length = text_len[0]
    score_scale = HEAD_DIM ** (-0.5)
    key_rows = jnp.concatenate([image_keys[0], text_keys[0]], 0)
    value_rows = jnp.concatenate([image_values[0], text_values[0]], 0)
    seq_count = lax.axis_size("seq")
    img_all = img_rows * seq_count
    unit_count = HEADS * img_rows
    head_span = min(HEADS, (unit_count - 1) // img_all + 2)
    slot_width = head_span * HEAD_DIM
    targets = jnp.arange(seq_count, dtype=jnp.int32)
    first_head = targets * unit_count // img_all
    slot_heads = first_head[:, None] + jnp.arange(head_span, dtype=jnp.int32)[None, :]

    def spread(rows):
        parts = []
        for target in range(seq_count):
            lead_head = target * unit_count // img_all
            for slot in range(lead_head, lead_head + head_span):
                head = min(slot, HEADS - 1)
                parts.append(rows[:, head * HEAD_DIM : (head + 1) * HEAD_DIM])
        return jnp.concatenate(parts, 1).reshape(rows.shape[0], seq_count, slot_width)

    query_in, key_in, value_in = (
        lax.all_to_all(spread(queries[0]), "seq", split_axis=1, concat_axis=1, tiled=True),
        lax.all_to_all(spread(key_rows), "seq", split_axis=1, concat_axis=1, tiled=True),
        lax.all_to_all(spread(value_rows), "seq", split_axis=1, concat_axis=1, tiled=True),
    )
    myself = lax.axis_index("seq")
    lead = myself * unit_count // img_all
    offset = myself * unit_count - lead * img_all
    query_flat = (
        query_in.reshape(img_rows, seq_count, head_span, HEAD_DIM)
        .transpose(2, 1, 0, 3)
        .reshape(head_span * img_all, HEAD_DIM)
    )
    query_units = lax.dynamic_slice_in_dim(query_flat, offset, unit_count, 0)
    unit_slot = (offset + jnp.arange(unit_count, dtype=jnp.int32)) // img_all
    slot_match = unit_slot[:, None] == jnp.arange(head_span, dtype=jnp.int32)[None, :]
    query_wide = jnp.where(
        slot_match[:, :, None], query_units[:, None, :], jnp.zeros((), jnp.bfloat16)
    ).reshape(unit_count, slot_width)
    key_count = both_rows * seq_count
    key_all = key_in.reshape(key_count, slot_width)
    value_all = value_in.reshape(key_count, slot_width)
    scores = (
        jnp.einsum("uw,kw->uk", query_wide, key_all, preferred_element_type=jnp.float32)
        * score_scale
    )
    local_row = jnp.arange(both_rows, dtype=jnp.int32)[:, None]
    text_slot = targets[None, :] * text_rows + local_row - img_rows
    valid = ((local_row < img_rows) | (text_slot < length)).reshape(-1)
    scores = jnp.where(valid[None, :], scores, -1e30)
    row_top = jnp.max(scores, -1, keepdims=True)
    weights = jnp.exp(scores - row_top)
    total = jnp.sum(weights, -1, keepdims=True)
    mixed = jnp.dot(
        weights.astype(jnp.bfloat16), value_all, preferred_element_type=jnp.float32
    ).reshape(unit_count, head_span, HEAD_DIM)
    picked = jnp.sum(jnp.where(slot_match[:, :, None], mixed, 0.0), 1)
    unit_out = (picked / total).astype(jnp.bfloat16)
    placed = lax.dynamic_update_slice_in_dim(
        jnp.zeros((head_span * img_all, HEAD_DIM), jnp.bfloat16), unit_out, offset, 0
    )
    going = (
        placed.reshape(head_span, seq_count, img_rows, HEAD_DIM)
        .transpose(2, 1, 0, 3)
        .reshape(img_rows, seq_count, slot_width)
    )
    coming = lax.all_to_all(going, "seq", split_axis=1, concat_axis=1, tiled=True)
    owner = (slot_heads[:, :, None] == jnp.arange(HEADS, dtype=jnp.int32)[None, None, :]).astype(
        jnp.bfloat16
    )
    attended = (
        jnp.einsum(
            "rjsd,jsh->rhd",
            coming.reshape(img_rows, seq_count, head_span, HEAD_DIM),
            owner,
            preferred_element_type=jnp.float32,
        )
        .reshape(img_rows, width)
        .astype(jnp.bfloat16)
    )
    mods = modulation[0]
    projected = jnp.dot(attended, w_out, preferred_element_type=jnp.float32)
    middle = hidden_in[0].astype(jnp.float32) + mods[0] * projected
    normed = (layer_norm(middle) * (1.0 + mods[2]) + mods[1]).astype(jnp.bfloat16)
    if seq_count == 16 and img_rows == 32:
        mlp_out = ffn_16(normed, w_up, w_down)
    else:
        mlp_out = ffn_any(normed, w_up, w_down)
    final = middle + mods[3] * mlp_out
    head_in = (layer_norm(final) * (1.0 + mods[5]) + mods[4]).astype(jnp.bfloat16)
    own_velocity = jnp.dot(head_in, w_final, preferred_element_type=jnp.float32)
    step_size = sigma_at(step_index[0] + 1) - sigma_at(step_index[0])
    scale_now = guidance[0]
    half_width = latent.shape[1]
    partner = partner_2(own_velocity, "cfg", 0)
    is_cond = lax.axis_index("cfg") == 0
    cond_part = jnp.where(is_cond, own_velocity, partner)
    uncond_part = jnp.where(is_cond, partner, own_velocity)
    velocity_full = uncond_part + scale_now * (cond_part - uncond_part)
    velocity = lax.dynamic_slice_in_dim(
        velocity_full, lax.axis_index("cfg") * half_width, half_width, 1
    )
    next_latent = latent + step_size * velocity
    return (velocity, next_latent)


def solution(mesh):
    in_specs = (
        P("cfg", "seq", None),
        P("cfg", "seq", None),
        P("cfg", "seq", None),
        P("cfg", "seq", None),
        P("cfg", "seq", None),
        P("cfg", "seq", None),
        P("cfg", None, None),
        P(),
        P(None, "seq"),
        P("seq", None),
        P(),
        P("seq", "cfg"),
        P("cfg"),
        P(),
        P(),
    )
    out_specs = (P("seq", "cfg"), P("seq", "cfg"))
    return jax.shard_map(body, mesh=mesh, in_specs=in_specs, out_specs=out_specs, check_vma=False)
```

```python
import functools

import jax
import jax.numpy as jnp
from jax import lax
from jax.experimental import pallas as pl
from jax.experimental.pallas import tpu as pltpu
from jax.sharding import PartitionSpec as P

HEADS = 38
HEAD_DIM = 64
STEPS = 28


shift_value = 3.0
norm_eps = 1e-06


def partner_2(value, axis, bit):
    mask = 2**bit
    pairs = [(source, source ^ mask) for source in range(lax.axis_size(axis))]
    return lax.ppermute(value, axis, pairs)


def layer_norm(values):
    centred = values - jnp.mean(values, -1, keepdims=True)
    return centred / jnp.sqrt(jnp.mean(centred * centred, -1, keepdims=True) + norm_eps)


def sigma_at(index):
    frac = 1.0 - index.astype(jnp.float32) / STEPS
    return shift_value * frac / (1.0 + (shift_value - 1.0) * frac)


def ffn_kernel(
    ca, norm_ref, up_ref, down_ref, out_ref, wu, wd, g, pf, pb, ry0, ry1, rx0, rx1, rxa, ryb, rz, s0, s1, s2,
    wsem, ssem, gsem, dsem, esem
):
    me = lax.axis_index("seq")
    mz = me // 4
    mx = lax.rem(me, 2)
    my = lax.rem(me // 2, 2)
    xn = mz * 4 + my * 2 + (1 - mx)
    yn = mz * 4 + (1 - my) * 2 + mx
    zs = [lax.rem(mz + k, 4) for k in range(4)]
    zn = [z * 4 + my * 2 + mx for z in zs]
    width = norm_ref.shape[1]
    cols = (pl.ds(0, ca), pl.ds(ca, width - ca))
    a, b = cols
    load_up = pltpu.make_async_copy(up_ref, wu, wsem.at[0])
    load_down = pltpu.make_async_copy(down_ref, wd, wsem.at[1])
    load_up.start()
    load_down.start()
    barrier = pltpu.get_barrier_semaphore()
    peers = (xn, yn, zn[1], zn[2], zn[3])
    for peer in peers:
        pl.semaphore_signal(barrier, inc=1, device_id={"seq": peer}, device_id_type=pl.DeviceIdType.MESH)
    sent = []

    def send(src, dst, recv, peer):
        copy = pltpu.make_async_remote_copy(
            src_ref=src, dst_ref=dst, send_sem=ssem.at[len(sent)], recv_sem=recv,
            device_id={"seq": peer}, device_id_type=pl.DeviceIdType.MESH,
        )
        copy.start()
        sent.append(copy)

    def arrived(dst, recv):
        pltpu.make_async_remote_copy(
            src_ref=dst, dst_ref=dst, send_sem=ssem.at[0], recv_sem=recv,
            device_id={"seq": xn}, device_id_type=pl.DeviceIdType.MESH,
        ).wait_recv()

    g[0, mz] = norm_ref[...]
    pl.semaphore_wait(barrier, len(peers))
    for k in (2, 1, 3):
        send(norm_ref, g.at[0, mz], gsem.at[0, mz], zn[k])
    send(norm_ref, g.at[1, mz], gsem.at[1, mz], xn)
    send(norm_ref, g.at[2, mz], gsem.at[2, mz], yn)
    for k in (1, 3, 2):
        z = zs[k]
        arrived(g.at[0, z], gsem.at[0, z])
        send(g.at[0, z], g.at[1, z], gsem.at[1, z], xn)
        send(g.at[0, z], g.at[2, z], gsem.at[2, z], yn)

    def up(q):
        rows = g[q].reshape(128, width)
        wide = lax.dot_general(rows, wu[...], (((1,), (1,)), ((), ())), preferred_element_type=jnp.float32)
        return jax.nn.gelu(wide, approximate=True).astype(jnp.bfloat16)

    def down(hid, half):
        made = jnp.dot(hid, wd[:, cols[half]], preferred_element_type=jnp.float32)
        return made.reshape(4, 32, made.shape[1])

    load_up.wait()
    for k in (0, 1):
        z = zs[k]
        arrived(g.at[1, z], gsem.at[1, z])
        send(g.at[1, z, :, a], g.at[3, z, :, a], gsem.at[3, z], yn)
        arrived(g.at[2, z], gsem.at[2, z])
        send(g.at[2, z, :, b], g.at[3, z, :, b], gsem.at[4, z], xn)
    hid0 = up(0)
    for k in (3, 2):
        z = zs[k]
        arrived(g.at[1, z], gsem.at[1, z])
        send(g.at[1, z, :, a], g.at[3, z, :, a], gsem.at[3, z], yn)
        arrived(g.at[2, z], gsem.at[2, z])
        send(g.at[2, z, :, b], g.at[3, z, :, b], gsem.at[4, z], xn)
    load_down.wait()
    hid1 = up(1)
    pb[1, :, :, b] = down(hid1, 1).astype(jnp.bfloat16)
    send(pb.at[1, :, :, b], rx0, dsem.at[0], xn)
    hid2 = up(2)
    pb[2, :, :, a] = down(hid2, 0).astype(jnp.bfloat16)
    send(pb.at[2, :, :, a], ry0, dsem.at[1], yn)
    pf[1, :, :, a] = down(hid1, 0)
    pf[2, :, :, b] = down(hid2, 1)
    pf[0, :, :, a] = down(hid0, 0)
    pf[0, :, :, b] = down(hid0, 1)
    for z in zs:
        arrived(g.at[3, z, :, a], gsem.at[3, z])
        arrived(g.at[3, z, :, b], gsem.at[4, z])
    hid3 = up(3)
    order = (2, 1, 3, 0)
    pb[3, :, :, a] = down(hid3, 0).astype(jnp.bfloat16)
    for k in order:
        send(pb.at[3, zs[k], :, a], ry1.at[zs[k]], esem.at[0, zs[k]], yn)
    pb[3, :, :, b] = down(hid3, 1).astype(jnp.bfloat16)
    for k in order:
        send(pb.at[3, zs[k], :, b], rx1.at[zs[k]], esem.at[1, zs[k]], xn)
    for k in order:
        z = zs[k]
        arrived(ry1.at[z], esem.at[0, z])
        s1[z] = (pf[1, z, :, a] + ry1[z].astype(jnp.float32)).astype(jnp.bfloat16)
        send(s1.at[z], rxa.at[z], esem.at[2, z], xn)
        arrived(rx1.at[z], esem.at[1, z])
        s2[z] = (pf[2, z, :, b] + rx1[z].astype(jnp.float32)).astype(jnp.bfloat16)
        send(s2.at[z], ryb.at[z], esem.at[3, z], yn)
    arrived(rx0, dsem.at[0])
    arrived(ry0, dsem.at[1])
    for k in order:
        z = zs[k]
        arrived(rxa.at[z], esem.at[2, z])
        arrived(ryb.at[z], esem.at[3, z])
        sum_a = pf[0, z, :, a] + ry0[z].astype(jnp.float32) + rxa[z].astype(jnp.float32)
        sum_b = pf[0, z, :, b] + rx0[z].astype(jnp.float32) + ryb[z].astype(jnp.float32)
        if k:
            s0[z, :, a] = sum_a.astype(jnp.bfloat16)
            s0[z, :, b] = sum_b.astype(jnp.bfloat16)
            send(s0.at[z], rz.at[mz], esem.at[4, mz], zn[k])
        else:
            out_ref[:, a] = sum_a
            out_ref[:, b] = sum_b
    for k in (1, 3, 2):
        arrived(rz.at[zs[k]], esem.at[4, zs[k]])
        out_ref[...] += rz[zs[k]].astype(jnp.float32)
    for copy in sent:
        copy.wait_send()


def ffn_16(normed, w_up, w_down):
    rows, width = normed.shape
    hidden = w_up.shape[1]
    ca = (width // 128 + 1) // 2 * 128
    cb = width - ca
    half = jnp.bfloat16
    return pl.pallas_call(
        functools.partial(ffn_kernel, ca),
        out_shape=jax.ShapeDtypeStruct((rows, width), jnp.float32),
        in_specs=[
            pl.BlockSpec(memory_space=pltpu.VMEM),
            pl.BlockSpec(memory_space=pl.ANY),
            pl.BlockSpec(memory_space=pl.ANY),
        ],
        out_specs=pl.BlockSpec(memory_space=pltpu.VMEM),
        scratch_shapes=[
            pltpu.VMEM((hidden, width), half),
            pltpu.VMEM((hidden, width), half),
            pltpu.VMEM((4, 4, rows, width), half),
            pltpu.VMEM((3, 4, rows, width), jnp.float32),
            pltpu.VMEM((4, 4, rows, width), half),
            pltpu.VMEM((4, rows, ca), half),
            pltpu.VMEM((4, rows, ca), half),
            pltpu.VMEM((4, rows, cb), half),
            pltpu.VMEM((4, rows, cb), half),
            pltpu.VMEM((4, rows, ca), half),
            pltpu.VMEM((4, rows, cb), half),
            pltpu.VMEM((4, rows, width), half),
            pltpu.VMEM((4, rows, width), half),
            pltpu.VMEM((4, rows, ca), half),
            pltpu.VMEM((4, rows, cb), half),
            pltpu.SemaphoreType.DMA((2,)),
            pltpu.SemaphoreType.DMA((48,)),
            pltpu.SemaphoreType.DMA((5, 4)),
            pltpu.SemaphoreType.DMA((2,)),
            pltpu.SemaphoreType.DMA((5, 4)),
        ],
        cost_estimate=pl.CostEstimate(
            flops=4 * 16 * rows * width * hidden, bytes_accessed=4 * width * hidden, transcendentals=16 * rows * hidden
        ),
        compiler_params=pltpu.CompilerParams(
            collective_id=0, has_side_effects=True, vmem_limit_bytes=44 * 2**20
        ),
    )(normed, w_up.T, w_down)


EXTRA = (5, 8, 6)
PAIR = 2 * HEAD_DIM


def attend_kernel(
    rows, st_ref, bias_ref, wo_ref, out_ref, wo, land, kb, vb, res, att, wsem, ssem, xsem, rsem, osem, asem, lsem
):
    me = lax.axis_index("seq")
    mesh_id = pl.DeviceIdType.MESH
    deep = rows * 3 + 16

    def lanes(pair):
        return pl.ds(pl.multiple_of(pair * PAIR, PAIR), PAIR)

    def peer_of(k):
        return lax.rem(me + k, 16)

    def remote(src, dst, sent, got, peer):
        return pltpu.make_async_remote_copy(
            src_ref=src, dst_ref=dst, send_sem=sent, recv_sem=got, device_id={"seq": peer}, device_id_type=mesh_id
        )

    load = pltpu.make_async_copy(wo_ref, wo, wsem.at[0])
    load.start()
    own = pltpu.make_async_copy(st_ref.at[:, lanes(me)], land.at[0, me], lsem.at[0])
    own.start()
    barrier = pltpu.get_barrier_semaphore()

    def greet(k, c):
        pl.semaphore_signal(barrier, inc=1, device_id={"seq": peer_of(k)}, device_id_type=mesh_id)
        return c

    lax.fori_loop(1, 16, greet, 0)
    pl.semaphore_wait(barrier, 15)

    def extra_in(e, owner):
        return remote(st_ref.at[:, lanes(16 + e)], land.at[1, me], xsem.at[e], rsem.at[1, me], owner)

    def extra_own(e):
        return pltpu.make_async_copy(st_ref.at[:, lanes(16 + e)], land.at[1, me], lsem.at[1])

    def pair_in(k):
        peer = peer_of(k)
        return remote(st_ref.at[:, lanes(peer)], land.at[0, me], ssem.at[k], rsem.at[0, me], peer)

    def go(k, c):
        pair_in(k).start()
        return c

    lax.fori_loop(1, 16, go, 0)
    for e, owner in enumerate(EXTRA):

        @pl.when(me != owner)
        def _():
            extra_in(e, owner).start()

        @pl.when(me == owner)
        def _():
            extra_own(e).start()

    def back(u, dst, pair):
        return remote(res.at[u, dst], att.at[:, lanes(pair)], osem.at[u, dst], asem.at[pair], dst)

    def unit(u, pair, local):
        def arrive(k, c):
            src = peer_of(k)
            remote(land.at[u, src], land.at[u, src], ssem.at[0], rsem.at[u, src], src).wait_recv()
            return c

        lax.fori_loop(1, 16, arrive, 0)
        local.wait()
        text = land[u, :, 3 * rows : deep, :].reshape(256, PAIR)
        slot = lax.broadcasted_iota(jnp.int32, (64, 256), 0)
        place = lax.broadcasted_iota(jnp.int32, (64, 256), 1)
        start = (slot >> 2) * 16 + (slot & 3)
        for kind, buf in ((0, kb), (1, vb)):
            pick = jnp.where(place == start + 4 * kind, 1.0, 0.0).astype(jnp.bfloat16)
            buf[512:576, :] = jnp.dot(pick, text, preferred_element_type=jnp.float32).astype(jnp.bfloat16)
            buf[0:512, :] = land[u, :, (kind + 1) * rows : (kind + 2) * rows, :].reshape(512, PAIR)
        low = lax.broadcasted_iota(jnp.int32, (4 * rows, PAIR), 1) < HEAD_DIM

        def chunk(c, carry):
            q = land[u, pl.ds(c * 4, 4), 0:rows, :].reshape(4 * rows, PAIR)
            made = []
            for head in range(2):
                mine = low if head == 0 else jnp.logical_not(low)
                q_one = jnp.where(mine, q, jnp.zeros_like(q))
                scores = lax.dot_general(
                    q_one, kb[...], (((1,), (1,)), ((), ())), preferred_element_type=jnp.float32
                ) * (HEAD_DIM ** (-0.5))
                scores = scores + bias_ref[...]
                top = jnp.max(scores, -1, keepdims=True)
                weights = jnp.exp(scores - top)
                total = jnp.sum(weights, -1, keepdims=True)
                mixed = jnp.dot(weights.astype(jnp.bfloat16), vb[...], preferred_element_type=jnp.float32)
                made.append(mixed / total)
            both = jnp.where(low, made[0], made[1]).astype(jnp.bfloat16)
            for j in range(4):
                dst = c * 4 + j
                res[u, dst] = both[j * rows : (j + 1) * rows, :]

                @pl.when(dst != me)
                def _():
                    back(u, dst, pair).start()

                @pl.when(dst == me)
                def _():
                    att[:, lanes(pair)] = both[j * rows : (j + 1) * rows, :]

            return carry

        lax.fori_loop(0, 4, chunk, 0)

    unit(0, me, own)
    for e, owner in enumerate(EXTRA):

        @pl.when(me == owner)
        def _():
            unit(1, 16 + e, extra_own(e))

    def home(pair, src):
        spot = att.at[:, lanes(pair)]
        remote(spot, spot, ssem.at[0], asem.at[pair], src).wait_recv()

    def collect(k, c):
        home(peer_of(k), peer_of(k))
        return c

    lax.fori_loop(1, 16, collect, 0)
    for e, owner in enumerate(EXTRA):

        @pl.when(me != owner)
        def _():
            home(16 + e, owner)

    load.wait()
    out_ref[...] = jnp.dot(att[...], wo[...], preferred_element_type=jnp.float32)

    def finish(k, c):
        pair_in(k).wait_send()
        back(0, peer_of(k), me).wait_send()
        return c

    lax.fori_loop(1, 16, finish, 0)
    for e, owner in enumerate(EXTRA):

        @pl.when(me != owner)
        def _():
            extra_in(e, owner).wait_send()

        @pl.when(me == owner)
        def _():
            def finish_extra(k, c):
                back(1, peer_of(k), 16 + e).wait_send()
                return c

            lax.fori_loop(1, 16, finish_extra, 0)


def attend_16(queries, image_keys, image_values, text_keys, text_values, w_out, length):
    rows, width = queries.shape
    half = jnp.bfloat16
    stacked = jnp.concatenate(
        [queries, image_keys, image_values, text_keys, text_values, jnp.zeros((8, width), half)], 0
    )
    deep = stacked.shape[0]
    key = jnp.arange(576, dtype=jnp.int32)
    bias = jnp.where(key - 512 < length, 0.0, -1e30).astype(jnp.float32)[None, :]
    pairs = width // PAIR
    return pl.pallas_call(
        functools.partial(attend_kernel, rows),
        out_shape=jax.ShapeDtypeStruct((rows, width), jnp.float32),
        in_specs=[
            pl.BlockSpec(memory_space=pltpu.VMEM),
            pl.BlockSpec(memory_space=pltpu.VMEM),
            pl.BlockSpec(memory_space=pl.ANY),
        ],
        out_specs=pl.BlockSpec(memory_space=pltpu.VMEM),
        scratch_shapes=[
            pltpu.VMEM((width, width), half),
            pltpu.VMEM((2, 16, deep, PAIR), half),
            pltpu.VMEM((576, PAIR), half),
            pltpu.VMEM((576, PAIR), half),
            pltpu.VMEM((2, 16, rows, PAIR), half),
            pltpu.VMEM((rows, width), half),
            pltpu.SemaphoreType.DMA((1,)),
            pltpu.SemaphoreType.DMA((16,)),
            pltpu.SemaphoreType.DMA((len(EXTRA),)),
            pltpu.SemaphoreType.DMA((2, 16)),
            pltpu.SemaphoreType.DMA((2, 16)),
            pltpu.SemaphoreType.DMA((pairs,)),
            pltpu.SemaphoreType.DMA((2,)),
        ],
        cost_estimate=pl.CostEstimate(
            flops=2 * rows * width * width, bytes_accessed=2 * width * width, transcendentals=2 * 512 * 576
        ),
        compiler_params=pltpu.CompilerParams(
            collective_id=1, has_side_effects=True, vmem_limit_bytes=44 * 2**20
        ),
    )(stacked, bias, w_out)


def ffn_any(normed, w_up, w_down):
    hidden_all = jax.nn.gelu(
        jnp.dot(
            lax.all_gather(normed, "seq", axis=0, tiled=True),
            w_up,
            preferred_element_type=jnp.float32,
        ),
        approximate=True,
    ).astype(jnp.bfloat16)
    mlp_out = lax.psum_scatter(
        jnp.dot(hidden_all, w_down, preferred_element_type=jnp.float32),
        "seq",
        scatter_dimension=0,
        tiled=True,
    )
    return mlp_out


def attend_any(queries, image_keys, image_values, text_keys, text_values, w_out, length):
    img_rows, width = queries.shape[1:]
    text_rows = text_keys.shape[1]
    both_rows = img_rows + text_rows
    score_scale = HEAD_DIM ** (-0.5)
    key_rows = jnp.concatenate([image_keys[0], text_keys[0]], 0)
    value_rows = jnp.concatenate([image_values[0], text_values[0]], 0)
    seq_count = lax.axis_size("seq")
    img_all = img_rows * seq_count
    unit_count = HEADS * img_rows
    head_span = min(HEADS, (unit_count - 1) // img_all + 2)
    slot_width = head_span * HEAD_DIM
    targets = jnp.arange(seq_count, dtype=jnp.int32)
    first_head = targets * unit_count // img_all
    slot_heads = first_head[:, None] + jnp.arange(head_span, dtype=jnp.int32)[None, :]

    def spread(rows):
        parts = []
        for target in range(seq_count):
            lead_head = target * unit_count // img_all
            for slot in range(lead_head, lead_head + head_span):
                head = min(slot, HEADS - 1)
                parts.append(rows[:, head * HEAD_DIM : (head + 1) * HEAD_DIM])
        return jnp.concatenate(parts, 1).reshape(rows.shape[0], seq_count, slot_width)

    query_in, key_in, value_in = (
        lax.all_to_all(spread(queries[0]), "seq", split_axis=1, concat_axis=1, tiled=True),
        lax.all_to_all(spread(key_rows), "seq", split_axis=1, concat_axis=1, tiled=True),
        lax.all_to_all(spread(value_rows), "seq", split_axis=1, concat_axis=1, tiled=True),
    )
    myself = lax.axis_index("seq")
    lead = myself * unit_count // img_all
    offset = myself * unit_count - lead * img_all
    query_flat = (
        query_in.reshape(img_rows, seq_count, head_span, HEAD_DIM)
        .transpose(2, 1, 0, 3)
        .reshape(head_span * img_all, HEAD_DIM)
    )
    query_units = lax.dynamic_slice_in_dim(query_flat, offset, unit_count, 0)
    unit_slot = (offset + jnp.arange(unit_count, dtype=jnp.int32)) // img_all
    slot_match = unit_slot[:, None] == jnp.arange(head_span, dtype=jnp.int32)[None, :]
    query_wide = jnp.where(
        slot_match[:, :, None], query_units[:, None, :], jnp.zeros((), jnp.bfloat16)
    ).reshape(unit_count, slot_width)
    key_count = both_rows * seq_count
    key_all = key_in.reshape(key_count, slot_width)
    value_all = value_in.reshape(key_count, slot_width)
    scores = (
        jnp.einsum("uw,kw->uk", query_wide, key_all, preferred_element_type=jnp.float32)
        * score_scale
    )
    local_row = jnp.arange(both_rows, dtype=jnp.int32)[:, None]
    text_slot = targets[None, :] * text_rows + local_row - img_rows
    valid = ((local_row < img_rows) | (text_slot < length)).reshape(-1)
    scores = jnp.where(valid[None, :], scores, -1e30)
    row_top = jnp.max(scores, -1, keepdims=True)
    weights = jnp.exp(scores - row_top)
    total = jnp.sum(weights, -1, keepdims=True)
    mixed = jnp.dot(
        weights.astype(jnp.bfloat16), value_all, preferred_element_type=jnp.float32
    ).reshape(unit_count, head_span, HEAD_DIM)
    picked = jnp.sum(jnp.where(slot_match[:, :, None], mixed, 0.0), 1)
    unit_out = (picked / total).astype(jnp.bfloat16)
    placed = lax.dynamic_update_slice_in_dim(
        jnp.zeros((head_span * img_all, HEAD_DIM), jnp.bfloat16), unit_out, offset, 0
    )
    going = (
        placed.reshape(head_span, seq_count, img_rows, HEAD_DIM)
        .transpose(2, 1, 0, 3)
        .reshape(img_rows, seq_count, slot_width)
    )
    coming = lax.all_to_all(going, "seq", split_axis=1, concat_axis=1, tiled=True)
    owner = (slot_heads[:, :, None] == jnp.arange(HEADS, dtype=jnp.int32)[None, None, :]).astype(
        jnp.bfloat16
    )
    attended = (
        jnp.einsum(
            "rjsd,jsh->rhd",
            coming.reshape(img_rows, seq_count, head_span, HEAD_DIM),
            owner,
            preferred_element_type=jnp.float32,
        )
        .reshape(img_rows, width)
        .astype(jnp.bfloat16)
    )
    return jnp.dot(attended, w_out, preferred_element_type=jnp.float32)


def body(
    queries,
    image_keys,
    image_values,
    text_keys,
    text_values,
    hidden_in,
    modulation,
    w_out,
    w_up,
    w_down,
    w_final,
    latent,
    text_len,
    step_index,
    guidance,
):
    img_rows = queries.shape[1]
    text_rows = text_keys.shape[1]
    width = queries.shape[2]
    length = text_len[0]
    seq_count = lax.axis_size("seq")
    if seq_count == 16 and (img_rows, text_rows, width) == (32, 4, 19 * PAIR):
        projected = attend_16(
            queries[0], image_keys[0], image_values[0], text_keys[0], text_values[0], w_out, length
        )
    else:
        projected = attend_any(queries, image_keys, image_values, text_keys, text_values, w_out, length)
    mods = modulation[0]
    middle = hidden_in[0].astype(jnp.float32) + mods[0] * projected
    normed = (layer_norm(middle) * (1.0 + mods[2]) + mods[1]).astype(jnp.bfloat16)
    if seq_count == 16 and img_rows == 32:
        mlp_out = ffn_16(normed, w_up, w_down)
    else:
        mlp_out = ffn_any(normed, w_up, w_down)
    final = middle + mods[3] * mlp_out
    head_in = (layer_norm(final) * (1.0 + mods[5]) + mods[4]).astype(jnp.bfloat16)
    own_velocity = jnp.dot(head_in, w_final, preferred_element_type=jnp.float32)
    step_size = sigma_at(step_index[0] + 1) - sigma_at(step_index[0])
    scale_now = guidance[0]
    half_width = latent.shape[1]
    partner = partner_2(own_velocity, "cfg", 0)
    is_cond = lax.axis_index("cfg") == 0
    cond_part = jnp.where(is_cond, own_velocity, partner)
    uncond_part = jnp.where(is_cond, partner, own_velocity)
    velocity_full = uncond_part + scale_now * (cond_part - uncond_part)
    velocity = lax.dynamic_slice_in_dim(
        velocity_full, lax.axis_index("cfg") * half_width, half_width, 1
    )
    next_latent = latent + step_size * velocity
    return (velocity, next_latent)


def solution(mesh):
    in_specs = (
        P("cfg", "seq", None),
        P("cfg", "seq", None),
        P("cfg", "seq", None),
        P("cfg", "seq", None),
        P("cfg", "seq", None),
        P("cfg", "seq", None),
        P("cfg", None, None),
        P(),
        P(None, "seq"),
        P("seq", None),
        P(),
        P("seq", "cfg"),
        P("cfg"),
        P(),
        P(),
    )
    out_specs = (P("seq", "cfg"), P("seq", "cfg"))
    return jax.shard_map(body, mesh=mesh, in_specs=in_specs, out_specs=out_specs, check_vma=False)
```

```python
import functools

import jax
import jax.numpy as jnp
from jax import lax
from jax.experimental import pallas as pl
from jax.experimental.pallas import tpu as pltpu
from jax.sharding import PartitionSpec as P

HEADS = 38
HEAD_DIM = 64
STEPS = 28


shift_value = 3.0
norm_eps = 1e-06


def partner_2(value, axis, bit):
    mask = 2**bit
    pairs = [(source, source ^ mask) for source in range(lax.axis_size(axis))]
    return lax.ppermute(value, axis, pairs)


def layer_norm(values):
    centred = values - jnp.mean(values, -1, keepdims=True)
    return centred / jnp.sqrt(jnp.mean(centred * centred, -1, keepdims=True) + norm_eps)


def sigma_at(index):
    frac = 1.0 - index.astype(jnp.float32) / STEPS
    return shift_value * frac / (1.0 + (shift_value - 1.0) * frac)


def ffn_kernel(
    ca, norm_ref, up_ref, down_ref, out_ref, wu, wd, g, pf, pb, ry0, ry1, rx0, rx1, rxa, ryb, rz, s0, s1, s2,
    wsem, ssem, gsem, dsem, esem
):
    me = lax.axis_index("seq")
    mz = me // 4
    mx = lax.rem(me, 2)
    my = lax.rem(me // 2, 2)
    xn = mz * 4 + my * 2 + (1 - mx)
    yn = mz * 4 + (1 - my) * 2 + mx
    zs = [mz, mz + 1 - 2 * lax.rem(mz, 2), lax.rem(mz + 2, 4), 3 - mz]
    zn = [z * 4 + my * 2 + mx for z in zs]
    width = norm_ref.shape[1]
    cols = (pl.ds(0, ca), pl.ds(ca, width - ca))
    a, b = cols
    load_up = pltpu.make_async_copy(up_ref, wu, wsem.at[0])
    load_down = pltpu.make_async_copy(down_ref, wd, wsem.at[1])
    load_up.start()
    load_down.start()
    barrier = pltpu.get_barrier_semaphore()
    peers = (xn, yn, zn[1], zn[2], zn[3])
    for peer in peers:
        pl.semaphore_signal(barrier, inc=1, device_id={"seq": peer}, device_id_type=pl.DeviceIdType.MESH)
    sent = []

    def send(src, dst, recv, peer):
        copy = pltpu.make_async_remote_copy(
            src_ref=src, dst_ref=dst, send_sem=ssem.at[len(sent)], recv_sem=recv,
            device_id={"seq": peer}, device_id_type=pl.DeviceIdType.MESH,
        )
        copy.start()
        sent.append(copy)

    def arrived(dst, recv):
        pltpu.make_async_remote_copy(
            src_ref=dst, dst_ref=dst, send_sem=ssem.at[0], recv_sem=recv,
            device_id={"seq": xn}, device_id_type=pl.DeviceIdType.MESH,
        ).wait_recv()

    g[0, mz] = norm_ref[...]
    pl.semaphore_wait(barrier, len(peers))
    for k in (1, 3, 2):
        send(norm_ref, g.at[0, mz], gsem.at[0, mz], zn[k])
    send(norm_ref, g.at[1, mz], gsem.at[1, mz], xn)
    send(norm_ref, g.at[2, mz], gsem.at[2, mz], yn)
    for k in (1, 3, 2):
        z = zs[k]
        arrived(g.at[0, z], gsem.at[0, z])
        send(g.at[0, z], g.at[1, z], gsem.at[1, z], xn)
        send(g.at[0, z], g.at[2, z], gsem.at[2, z], yn)

    def up(q):
        rows = g[q].reshape(128, width)
        wide = lax.dot_general(rows, wu[...], (((1,), (1,)), ((), ())), preferred_element_type=jnp.float32)
        return jax.nn.gelu(wide, approximate=True).astype(jnp.bfloat16)

    def down(hid, half):
        made = jnp.dot(hid, wd[:, cols[half]], preferred_element_type=jnp.float32)
        return made.reshape(4, 32, made.shape[1])

    load_up.wait()
    for k in (0, 1):
        z = zs[k]
        arrived(g.at[1, z], gsem.at[1, z])
        send(g.at[1, z, :, a], g.at[3, z, :, a], gsem.at[3, z], yn)
        arrived(g.at[2, z], gsem.at[2, z])
        send(g.at[2, z, :, b], g.at[3, z, :, b], gsem.at[4, z], xn)
    hid0 = up(0)
    for k in (3, 2):
        z = zs[k]
        arrived(g.at[1, z], gsem.at[1, z])
        send(g.at[1, z, :, a], g.at[3, z, :, a], gsem.at[3, z], yn)
        arrived(g.at[2, z], gsem.at[2, z])
        send(g.at[2, z, :, b], g.at[3, z, :, b], gsem.at[4, z], xn)
    load_down.wait()
    hid1 = up(1)
    pb[1, :, :, b] = down(hid1, 1).astype(jnp.bfloat16)
    send(pb.at[1, :, :, b], rx0, dsem.at[0], xn)
    hid2 = up(2)
    pb[2, :, :, a] = down(hid2, 0).astype(jnp.bfloat16)
    send(pb.at[2, :, :, a], ry0, dsem.at[1], yn)
    pf[1, :, :, a] = down(hid1, 0)
    pf[2, :, :, b] = down(hid2, 1)
    for z in zs:
        arrived(g.at[3, z, :, a], gsem.at[3, z])
        arrived(g.at[3, z, :, b], gsem.at[4, z])
    hid3 = up(3)
    order = (2, 1, 3, 0)
    pb[3, :, :, a] = down(hid3, 0).astype(jnp.bfloat16)
    for k in order:
        send(pb.at[3, zs[k], :, a], ry1.at[zs[k]], esem.at[0, zs[k]], yn)
    pb[3, :, :, b] = down(hid3, 1).astype(jnp.bfloat16)
    for k in order:
        send(pb.at[3, zs[k], :, b], rx1.at[zs[k]], esem.at[1, zs[k]], xn)
    pf[0, :, :, a] = down(hid0, 0)
    pf[0, :, :, b] = down(hid0, 1)
    for k in order:
        z = zs[k]
        arrived(ry1.at[z], esem.at[0, z])
        s1[z] = (pf[1, z, :, a] + ry1[z].astype(jnp.float32)).astype(jnp.bfloat16)
        send(s1.at[z], rxa.at[z], esem.at[2, z], xn)
        arrived(rx1.at[z], esem.at[1, z])
        s2[z] = (pf[2, z, :, b] + rx1[z].astype(jnp.float32)).astype(jnp.bfloat16)
        send(s2.at[z], ryb.at[z], esem.at[3, z], yn)
    arrived(rx0, dsem.at[0])
    arrived(ry0, dsem.at[1])
    for k in order:
        z = zs[k]
        arrived(rxa.at[z], esem.at[2, z])
        arrived(ryb.at[z], esem.at[3, z])
        sum_a = pf[0, z, :, a] + ry0[z].astype(jnp.float32) + rxa[z].astype(jnp.float32)
        sum_b = pf[0, z, :, b] + rx0[z].astype(jnp.float32) + ryb[z].astype(jnp.float32)
        if k:
            s0[z, :, a] = sum_a.astype(jnp.bfloat16)
            s0[z, :, b] = sum_b.astype(jnp.bfloat16)
            send(s0.at[z], rz.at[mz], esem.at[4, mz], zn[k])
        else:
            out_ref[:, a] = sum_a
            out_ref[:, b] = sum_b
    for k in (1, 3, 2):
        arrived(rz.at[zs[k]], esem.at[4, zs[k]])
        out_ref[...] += rz[zs[k]].astype(jnp.float32)
    for copy in sent:
        copy.wait_send()


def ffn_16(normed, w_up, w_down):
    rows, width = normed.shape
    hidden = w_up.shape[1]
    ca = (width // 128 + 1) // 2 * 128
    cb = width - ca
    half = jnp.bfloat16
    return pl.pallas_call(
        functools.partial(ffn_kernel, ca),
        out_shape=jax.ShapeDtypeStruct((rows, width), jnp.float32),
        in_specs=[
            pl.BlockSpec(memory_space=pltpu.VMEM),
            pl.BlockSpec(memory_space=pl.ANY),
            pl.BlockSpec(memory_space=pl.ANY),
        ],
        out_specs=pl.BlockSpec(memory_space=pltpu.VMEM),
        scratch_shapes=[
            pltpu.VMEM((hidden, width), half),
            pltpu.VMEM((hidden, width), half),
            pltpu.VMEM((4, 4, rows, width), half),
            pltpu.VMEM((3, 4, rows, width), jnp.float32),
            pltpu.VMEM((4, 4, rows, width), half),
            pltpu.VMEM((4, rows, ca), half),
            pltpu.VMEM((4, rows, ca), half),
            pltpu.VMEM((4, rows, cb), half),
            pltpu.VMEM((4, rows, cb), half),
            pltpu.VMEM((4, rows, ca), half),
            pltpu.VMEM((4, rows, cb), half),
            pltpu.VMEM((4, rows, width), half),
            pltpu.VMEM((4, rows, width), half),
            pltpu.VMEM((4, rows, ca), half),
            pltpu.VMEM((4, rows, cb), half),
            pltpu.SemaphoreType.DMA((2,)),
            pltpu.SemaphoreType.DMA((48,)),
            pltpu.SemaphoreType.DMA((5, 4)),
            pltpu.SemaphoreType.DMA((2,)),
            pltpu.SemaphoreType.DMA((5, 4)),
        ],
        cost_estimate=pl.CostEstimate(
            flops=4 * 16 * rows * width * hidden, bytes_accessed=4 * width * hidden, transcendentals=16 * rows * hidden
        ),
        compiler_params=pltpu.CompilerParams(
            collective_id=0, has_side_effects=True, vmem_limit_bytes=44 * 2**20
        ),
    )(normed, w_up.T, w_down)


EXTRA = (5, 8, 6)
PAIR = 2 * HEAD_DIM


def attend_kernel(
    rows, q_ref, k_ref, v_ref, text_ref, bias_ref, wo_ref, out_ref, st_ref, wo, land, kb, vb, res, att, wsem, ssem, xsem, rsem, osem, asem, lsem
):
    me = lax.axis_index("seq")
    mesh_id = pl.DeviceIdType.MESH
    deep = rows * 3 + 16

    def lanes(pair):
        return pl.ds(pl.multiple_of(pair * PAIR, PAIR), PAIR)

    def peer_of(k):
        return lax.rem(me + k, 16)

    def remote(src, dst, sent, got, peer):
        return pltpu.make_async_remote_copy(
            src_ref=src, dst_ref=dst, send_sem=sent, recv_sem=got, device_id={"seq": peer}, device_id_type=mesh_id
        )

    stack = [
        pltpu.make_async_copy(ref, st_ref.at[pl.ds(i * rows, ref.shape[0])], wsem.at[i + 1])
        for i, ref in enumerate((q_ref, k_ref, v_ref, text_ref))
    ]
    for copy in stack:
        copy.start()
    load = pltpu.make_async_copy(wo_ref, wo, wsem.at[0])
    load.start()
    own = pltpu.make_async_copy(st_ref.at[:, lanes(me)], land.at[0, me], lsem.at[0])
    barrier = pltpu.get_barrier_semaphore()

    def greet(k, c):
        pl.semaphore_signal(barrier, inc=1, device_id={"seq": peer_of(k)}, device_id_type=mesh_id)
        return c

    lax.fori_loop(1, 16, greet, 0)
    for copy in stack:
        copy.wait()
    own.start()
    pl.semaphore_wait(barrier, 15)

    def extra_in(e, owner):
        return remote(st_ref.at[:, lanes(16 + e)], land.at[1, me], xsem.at[e], rsem.at[1, me], owner)

    def extra_own(e):
        return pltpu.make_async_copy(st_ref.at[:, lanes(16 + e)], land.at[1, me], lsem.at[1])

    def pair_in(k):
        peer = peer_of(k)
        return remote(st_ref.at[:, lanes(peer)], land.at[0, me], ssem.at[k], rsem.at[0, me], peer)

    def go(k, c):
        pair_in(k).start()
        return c

    lax.fori_loop(1, 16, go, 0)
    for e, owner in enumerate(EXTRA):

        @pl.when(me != owner)
        def _():
            extra_in(e, owner).start()

        @pl.when(me == owner)
        def _():
            extra_own(e).start()

    def back(u, dst, pair):
        return remote(res.at[u, dst], att.at[:, lanes(pair)], osem.at[u, dst], asem.at[pair], dst)

    def unit(u, pair, local):
        def arrive(k, c):
            src = peer_of(k)
            remote(land.at[u, src], land.at[u, src], ssem.at[0], rsem.at[u, src], src).wait_recv()
            return c

        lax.fori_loop(1, 16, arrive, 0)
        local.wait()
        text = land[u, :, 3 * rows : deep, :].reshape(256, PAIR)
        slot = lax.broadcasted_iota(jnp.int32, (64, 256), 0)
        place = lax.broadcasted_iota(jnp.int32, (64, 256), 1)
        start = (slot >> 2) * 16 + (slot & 3)
        for kind, buf in ((0, kb), (1, vb)):
            pick = jnp.where(place == start + 4 * kind, 1.0, 0.0).astype(jnp.bfloat16)
            buf[512:576, :] = jnp.dot(pick, text, preferred_element_type=jnp.float32).astype(jnp.bfloat16)
            buf[0:512, :] = land[u, :, (kind + 1) * rows : (kind + 2) * rows, :].reshape(512, PAIR)
        low = lax.broadcasted_iota(jnp.int32, (4 * rows, PAIR), 1) < HEAD_DIM

        def chunk(c, carry):
            made = []
            for part in range(2):
                q = land[u, pl.ds(c * 8 + part * 4, 4), 0:rows, :].reshape(4 * rows, PAIR)
                none = jnp.zeros_like(q)
                q_two = jnp.concatenate([jnp.where(low, q, none), jnp.where(low, none, q)], 0)
                scores = lax.dot_general(
                    q_two, kb[...], (((1,), (1,)), ((), ())), preferred_element_type=jnp.float32
                ) * (HEAD_DIM ** (-0.5))
                scores = scores + bias_ref[...]
                top = jnp.max(scores, -1, keepdims=True)
                weights = jnp.exp(scores - top)
                total = jnp.sum(weights, -1, keepdims=True)
                mixed = jnp.dot(weights.astype(jnp.bfloat16), vb[...], preferred_element_type=jnp.float32) / total
                made.append(jnp.where(low, mixed[: 4 * rows], mixed[4 * rows :]).astype(jnp.bfloat16))
            both = jnp.concatenate(made, 0)
            for j in range(8):
                dst = c * 8 + j
                res[u, dst] = both[j * rows : (j + 1) * rows, :]

                @pl.when(dst != me)
                def _():
                    back(u, dst, pair).start()

                @pl.when(dst == me)
                def _():
                    att[:, lanes(pair)] = both[j * rows : (j + 1) * rows, :]

            return carry

        lax.fori_loop(0, 2, chunk, 0)

    unit(0, me, own)
    for e, owner in enumerate(EXTRA):

        @pl.when(me == owner)
        def _():
            unit(1, 16 + e, extra_own(e))

    def home(pair, src):
        spot = att.at[:, lanes(pair)]
        remote(spot, spot, ssem.at[0], asem.at[pair], src).wait_recv()

    def collect(k, c):
        home(peer_of(k), peer_of(k))
        return c

    lax.fori_loop(1, 16, collect, 0)
    for e, owner in enumerate(EXTRA):

        @pl.when(me != owner)
        def _():
            home(16 + e, owner)

    load.wait()
    out_ref[...] = jnp.dot(att[...], wo[...], preferred_element_type=jnp.float32)

    def finish(k, c):
        pair_in(k).wait_send()
        back(0, peer_of(k), me).wait_send()
        return c

    lax.fori_loop(1, 16, finish, 0)
    for e, owner in enumerate(EXTRA):

        @pl.when(me != owner)
        def _():
            extra_in(e, owner).wait_send()

        @pl.when(me == owner)
        def _():
            def finish_extra(k, c):
                back(1, peer_of(k), 16 + e).wait_send()
                return c

            lax.fori_loop(1, 16, finish_extra, 0)


def attend_16(queries, image_keys, image_values, text_keys, text_values, w_out, length):
    rows, width = queries.shape
    half = jnp.bfloat16
    text = jnp.concatenate([text_keys, text_values, jnp.zeros((8, width), half)], 0)
    deep = 3 * rows + text.shape[0]
    key = jnp.arange(576, dtype=jnp.int32)
    bias = jnp.where(key - 512 < length, 0.0, -1e30).astype(jnp.float32)[None, :]
    pairs = width // PAIR
    return pl.pallas_call(
        functools.partial(attend_kernel, rows),
        out_shape=jax.ShapeDtypeStruct((rows, width), jnp.float32),
        in_specs=[
            pl.BlockSpec(memory_space=pl.ANY),
            pl.BlockSpec(memory_space=pl.ANY),
            pl.BlockSpec(memory_space=pl.ANY),
            pl.BlockSpec(memory_space=pl.ANY),
            pl.BlockSpec(memory_space=pltpu.VMEM),
            pl.BlockSpec(memory_space=pl.ANY),
        ],
        out_specs=pl.BlockSpec(memory_space=pltpu.VMEM),
        scratch_shapes=[
            pltpu.VMEM((deep, width), half),
            pltpu.VMEM((width, width), half),
            pltpu.VMEM((2, 16, deep, PAIR), half),
            pltpu.VMEM((576, PAIR), half),
            pltpu.VMEM((576, PAIR), half),
            pltpu.VMEM((2, 16, rows, PAIR), half),
            pltpu.VMEM((rows, width), half),
            pltpu.SemaphoreType.DMA((5,)),
            pltpu.SemaphoreType.DMA((16,)),
            pltpu.SemaphoreType.DMA((len(EXTRA),)),
            pltpu.SemaphoreType.DMA((2, 16)),
            pltpu.SemaphoreType.DMA((2, 16)),
            pltpu.SemaphoreType.DMA((pairs,)),
            pltpu.SemaphoreType.DMA((2,)),
        ],
        cost_estimate=pl.CostEstimate(
            flops=2 * rows * width * width, bytes_accessed=2 * width * width, transcendentals=2 * 512 * 576
        ),
        compiler_params=pltpu.CompilerParams(
            collective_id=1, has_side_effects=True, vmem_limit_bytes=44 * 2**20
        ),
    )(queries, image_keys, image_values, text, bias, w_out)


def ffn_any(normed, w_up, w_down):
    hidden_all = jax.nn.gelu(
        jnp.dot(
            lax.all_gather(normed, "seq", axis=0, tiled=True),
            w_up,
            preferred_element_type=jnp.float32,
        ),
        approximate=True,
    ).astype(jnp.bfloat16)
    mlp_out = lax.psum_scatter(
        jnp.dot(hidden_all, w_down, preferred_element_type=jnp.float32),
        "seq",
        scatter_dimension=0,
        tiled=True,
    )
    return mlp_out


def attend_any(queries, image_keys, image_values, text_keys, text_values, w_out, length):
    img_rows, width = queries.shape[1:]
    text_rows = text_keys.shape[1]
    both_rows = img_rows + text_rows
    score_scale = HEAD_DIM ** (-0.5)
    key_rows = jnp.concatenate([image_keys[0], text_keys[0]], 0)
    value_rows = jnp.concatenate([image_values[0], text_values[0]], 0)
    seq_count = lax.axis_size("seq")
    img_all = img_rows * seq_count
    unit_count = HEADS * img_rows
    head_span = min(HEADS, (unit_count - 1) // img_all + 2)
    slot_width = head_span * HEAD_DIM
    targets = jnp.arange(seq_count, dtype=jnp.int32)
    first_head = targets * unit_count // img_all
    slot_heads = first_head[:, None] + jnp.arange(head_span, dtype=jnp.int32)[None, :]

    def spread(rows):
        parts = []
        for target in range(seq_count):
            lead_head = target * unit_count // img_all
            for slot in range(lead_head, lead_head + head_span):
                head = min(slot, HEADS - 1)
                parts.append(rows[:, head * HEAD_DIM : (head + 1) * HEAD_DIM])
        return jnp.concatenate(parts, 1).reshape(rows.shape[0], seq_count, slot_width)

    query_in, key_in, value_in = (
        lax.all_to_all(spread(queries[0]), "seq", split_axis=1, concat_axis=1, tiled=True),
        lax.all_to_all(spread(key_rows), "seq", split_axis=1, concat_axis=1, tiled=True),
        lax.all_to_all(spread(value_rows), "seq", split_axis=1, concat_axis=1, tiled=True),
    )
    myself = lax.axis_index("seq")
    lead = myself * unit_count // img_all
    offset = myself * unit_count - lead * img_all
    query_flat = (
        query_in.reshape(img_rows, seq_count, head_span, HEAD_DIM)
        .transpose(2, 1, 0, 3)
        .reshape(head_span * img_all, HEAD_DIM)
    )
    query_units = lax.dynamic_slice_in_dim(query_flat, offset, unit_count, 0)
    unit_slot = (offset + jnp.arange(unit_count, dtype=jnp.int32)) // img_all
    slot_match = unit_slot[:, None] == jnp.arange(head_span, dtype=jnp.int32)[None, :]
    query_wide = jnp.where(
        slot_match[:, :, None], query_units[:, None, :], jnp.zeros((), jnp.bfloat16)
    ).reshape(unit_count, slot_width)
    key_count = both_rows * seq_count
    key_all = key_in.reshape(key_count, slot_width)
    value_all = value_in.reshape(key_count, slot_width)
    scores = (
        jnp.einsum("uw,kw->uk", query_wide, key_all, preferred_element_type=jnp.float32)
        * score_scale
    )
    local_row = jnp.arange(both_rows, dtype=jnp.int32)[:, None]
    text_slot = targets[None, :] * text_rows + local_row - img_rows
    valid = ((local_row < img_rows) | (text_slot < length)).reshape(-1)
    scores = jnp.where(valid[None, :], scores, -1e30)
    row_top = jnp.max(scores, -1, keepdims=True)
    weights = jnp.exp(scores - row_top)
    total = jnp.sum(weights, -1, keepdims=True)
    mixed = jnp.dot(
        weights.astype(jnp.bfloat16), value_all, preferred_element_type=jnp.float32
    ).reshape(unit_count, head_span, HEAD_DIM)
    picked = jnp.sum(jnp.where(slot_match[:, :, None], mixed, 0.0), 1)
    unit_out = (picked / total).astype(jnp.bfloat16)
    placed = lax.dynamic_update_slice_in_dim(
        jnp.zeros((head_span * img_all, HEAD_DIM), jnp.bfloat16), unit_out, offset, 0
    )
    going = (
        placed.reshape(head_span, seq_count, img_rows, HEAD_DIM)
        .transpose(2, 1, 0, 3)
        .reshape(img_rows, seq_count, slot_width)
    )
    coming = lax.all_to_all(going, "seq", split_axis=1, concat_axis=1, tiled=True)
    owner = (slot_heads[:, :, None] == jnp.arange(HEADS, dtype=jnp.int32)[None, None, :]).astype(
        jnp.bfloat16
    )
    attended = (
        jnp.einsum(
            "rjsd,jsh->rhd",
            coming.reshape(img_rows, seq_count, head_span, HEAD_DIM),
            owner,
            preferred_element_type=jnp.float32,
        )
        .reshape(img_rows, width)
        .astype(jnp.bfloat16)
    )
    return jnp.dot(attended, w_out, preferred_element_type=jnp.float32)


def body(
    queries,
    image_keys,
    image_values,
    text_keys,
    text_values,
    hidden_in,
    modulation,
    w_out,
    w_up,
    w_down,
    w_final,
    latent,
    text_len,
    step_index,
    guidance,
):
    img_rows = queries.shape[1]
    text_rows = text_keys.shape[1]
    width = queries.shape[2]
    length = text_len[0]
    seq_count = lax.axis_size("seq")
    if seq_count == 16 and (img_rows, text_rows, width) == (32, 4, 19 * PAIR):
        projected = attend_16(
            queries[0], image_keys[0], image_values[0], text_keys[0], text_values[0], w_out, length
        )
    else:
        projected = attend_any(queries, image_keys, image_values, text_keys, text_values, w_out, length)
    mods = modulation[0]
    middle = hidden_in[0].astype(jnp.float32) + mods[0] * projected
    normed = (layer_norm(middle) * (1.0 + mods[2]) + mods[1]).astype(jnp.bfloat16)
    if seq_count == 16 and img_rows == 32:
        mlp_out = ffn_16(normed, w_up, w_down)
    else:
        mlp_out = ffn_any(normed, w_up, w_down)
    final = middle + mods[3] * mlp_out
    head_in = (layer_norm(final) * (1.0 + mods[5]) + mods[4]).astype(jnp.bfloat16)
    own_velocity = jnp.dot(head_in, w_final, preferred_element_type=jnp.float32)
    step_size = sigma_at(step_index[0] + 1) - sigma_at(step_index[0])
    scale_now = guidance[0]
    half_width = latent.shape[1]
    partner = partner_2(own_velocity, "cfg", 0)
    is_cond = lax.axis_index("cfg") == 0
    cond_part = jnp.where(is_cond, own_velocity, partner)
    uncond_part = jnp.where(is_cond, partner, own_velocity)
    velocity_full = uncond_part + scale_now * (cond_part - uncond_part)
    velocity = lax.dynamic_slice_in_dim(
        velocity_full, lax.axis_index("cfg") * half_width, half_width, 1
    )
    next_latent = latent + step_size * velocity
    return (velocity, next_latent)


def solution(mesh):
    in_specs = (
        P("cfg", "seq", None),
        P("cfg", "seq", None),
        P("cfg", "seq", None),
        P("cfg", "seq", None),
        P("cfg", "seq", None),
        P("cfg", "seq", None),
        P("cfg", None, None),
        P(),
        P(None, "seq"),
        P("seq", None),
        P(),
        P("seq", "cfg"),
        P("cfg"),
        P(),
        P(),
    )
    out_specs = (P("seq", "cfg"), P("seq", "cfg"))
    return jax.shard_map(body, mesh=mesh, in_specs=in_specs, out_specs=out_specs, check_vma=False)
```

```python
import functools

import jax
import jax.numpy as jnp
from jax import lax
from jax.experimental import pallas as pl
from jax.experimental.pallas import tpu as pltpu
from jax.sharding import PartitionSpec as P

HEADS = 38
HEAD_DIM = 64
STEPS = 28


shift_value = 3.0
norm_eps = 1e-06


def partner_2(value, axis, bit):
    mask = 2**bit
    pairs = [(source, source ^ mask) for source in range(lax.axis_size(axis))]
    return lax.ppermute(value, axis, pairs)


def layer_norm(values):
    centred = values - jnp.mean(values, -1, keepdims=True)
    return centred / jnp.sqrt(jnp.mean(centred * centred, -1, keepdims=True) + norm_eps)


def sigma_at(index):
    frac = 1.0 - index.astype(jnp.float32) / STEPS
    return shift_value * frac / (1.0 + (shift_value - 1.0) * frac)


def ffn_kernel(
    ca, norm_ref, up_ref, down_ref, out_ref, wu, wd, g, pf, pb, ry0, ry1, rx0, rx1, rxa, ryb, rz, s0, s1, s2,
    wsem, ssem, gsem, dsem, esem
):
    me = lax.axis_index("seq")
    mz = me // 4
    mx = lax.rem(me, 2)
    my = lax.rem(me // 2, 2)
    xn = mz * 4 + my * 2 + (1 - mx)
    yn = mz * 4 + (1 - my) * 2 + mx
    zs = [mz, mz + 1 - 2 * lax.rem(mz, 2), lax.rem(mz + 2, 4), 3 - mz]
    zn = [z * 4 + my * 2 + mx for z in zs]
    width = norm_ref.shape[1]
    cols = (pl.ds(0, ca), pl.ds(ca, width - ca))
    a, b = cols
    load_up = pltpu.make_async_copy(up_ref, wu, wsem.at[0])
    load_down = pltpu.make_async_copy(down_ref, wd, wsem.at[1])
    load_up.start()
    load_down.start()
    barrier = pltpu.get_barrier_semaphore()
    peers = (xn, yn, zn[1], zn[2], zn[3])
    for peer in peers:
        pl.semaphore_signal(barrier, inc=1, device_id={"seq": peer}, device_id_type=pl.DeviceIdType.MESH)
    sent = []

    def send(src, dst, recv, peer):
        copy = pltpu.make_async_remote_copy(
            src_ref=src, dst_ref=dst, send_sem=ssem.at[len(sent)], recv_sem=recv,
            device_id={"seq": peer}, device_id_type=pl.DeviceIdType.MESH,
        )
        copy.start()
        sent.append(copy)

    def arrived(dst, recv):
        pltpu.make_async_remote_copy(
            src_ref=dst, dst_ref=dst, send_sem=ssem.at[0], recv_sem=recv,
            device_id={"seq": xn}, device_id_type=pl.DeviceIdType.MESH,
        ).wait_recv()

    g[0, mz] = norm_ref[...]
    pl.semaphore_wait(barrier, len(peers))
    for k in (1, 3, 2):
        send(norm_ref, g.at[0, mz], gsem.at[0, mz], zn[k])
    send(norm_ref, g.at[1, mz], gsem.at[1, mz], xn)
    send(norm_ref, g.at[2, mz], gsem.at[2, mz], yn)
    for k in (1, 3, 2):
        z = zs[k]
        arrived(g.at[0, z], gsem.at[0, z])
        send(g.at[0, z], g.at[1, z], gsem.at[1, z], xn)
        send(g.at[0, z], g.at[2, z], gsem.at[2, z], yn)

    def up(q):
        rows = g[q].reshape(128, width)
        wide = lax.dot_general(rows, wu[...], (((1,), (1,)), ((), ())), preferred_element_type=jnp.float32)
        return jax.nn.gelu(wide, approximate=True).astype(jnp.bfloat16)

    def down(hid, half):
        made = jnp.dot(hid, wd[:, cols[half]], preferred_element_type=jnp.float32)
        return made.reshape(4, 32, made.shape[1])

    load_up.wait()
    for k in (0, 1):
        z = zs[k]
        arrived(g.at[1, z], gsem.at[1, z])
        send(g.at[1, z, :, a], g.at[3, z, :, a], gsem.at[3, z], yn)
        arrived(g.at[2, z], gsem.at[2, z])
        send(g.at[2, z, :, b], g.at[3, z, :, b], gsem.at[4, z], xn)
    hid0 = up(0)
    for k in (3, 2):
        z = zs[k]
        arrived(g.at[1, z], gsem.at[1, z])
        send(g.at[1, z, :, a], g.at[3, z, :, a], gsem.at[3, z], yn)
        arrived(g.at[2, z], gsem.at[2, z])
        send(g.at[2, z, :, b], g.at[3, z, :, b], gsem.at[4, z], xn)
    load_down.wait()
    hid1 = up(1)
    pb[1, :, :, b] = down(hid1, 1).astype(jnp.bfloat16)
    send(pb.at[1, :, :, b], rx0, dsem.at[0], xn)
    hid2 = up(2)
    pb[2, :, :, a] = down(hid2, 0).astype(jnp.bfloat16)
    send(pb.at[2, :, :, a], ry0, dsem.at[1], yn)
    pf[1, :, :, a] = down(hid1, 0)
    pf[2, :, :, b] = down(hid2, 1)
    for z in zs:
        arrived(g.at[3, z, :, a], gsem.at[3, z])
        arrived(g.at[3, z, :, b], gsem.at[4, z])
    hid3 = up(3)
    order = (2, 1, 3, 0)
    pb[3, :, :, a] = down(hid3, 0).astype(jnp.bfloat16)
    for k in order:
        send(pb.at[3, zs[k], :, a], ry1.at[zs[k]], esem.at[0, zs[k]], yn)
    pb[3, :, :, b] = down(hid3, 1).astype(jnp.bfloat16)
    for k in order:
        send(pb.at[3, zs[k], :, b], rx1.at[zs[k]], esem.at[1, zs[k]], xn)
    pf[0, :, :, a] = down(hid0, 0)
    pf[0, :, :, b] = down(hid0, 1)
    for k in order:
        z = zs[k]
        arrived(ry1.at[z], esem.at[0, z])
        s1[z] = (pf[1, z, :, a] + ry1[z].astype(jnp.float32)).astype(jnp.bfloat16)
        send(s1.at[z], rxa.at[z], esem.at[2, z], xn)
        arrived(rx1.at[z], esem.at[1, z])
        s2[z] = (pf[2, z, :, b] + rx1[z].astype(jnp.float32)).astype(jnp.bfloat16)
        send(s2.at[z], ryb.at[z], esem.at[3, z], yn)
    arrived(rx0, dsem.at[0])
    arrived(ry0, dsem.at[1])
    for k in order:
        z = zs[k]
        arrived(rxa.at[z], esem.at[2, z])
        arrived(ryb.at[z], esem.at[3, z])
        sum_a = pf[0, z, :, a] + ry0[z].astype(jnp.float32) + rxa[z].astype(jnp.float32)
        sum_b = pf[0, z, :, b] + rx0[z].astype(jnp.float32) + ryb[z].astype(jnp.float32)
        if k:
            s0[z, :, a] = sum_a.astype(jnp.bfloat16)
            s0[z, :, b] = sum_b.astype(jnp.bfloat16)
            send(s0.at[z], rz.at[mz], esem.at[4, mz], zn[k])
        else:
            out_ref[:, a] = sum_a
            out_ref[:, b] = sum_b
    for k in (1, 3, 2):
        arrived(rz.at[zs[k]], esem.at[4, zs[k]])
        out_ref[...] += rz[zs[k]].astype(jnp.float32)
    for copy in sent:
        copy.wait_send()


def ffn_16(normed, w_up, w_down):
    rows, width = normed.shape
    hidden = w_up.shape[1]
    ca = (width // 128 + 1) // 2 * 128
    cb = width - ca
    half = jnp.bfloat16
    return pl.pallas_call(
        functools.partial(ffn_kernel, ca),
        out_shape=jax.ShapeDtypeStruct((rows, width), jnp.float32),
        in_specs=[
            pl.BlockSpec(memory_space=pltpu.VMEM),
            pl.BlockSpec(memory_space=pl.ANY),
            pl.BlockSpec(memory_space=pl.ANY),
        ],
        out_specs=pl.BlockSpec(memory_space=pltpu.VMEM),
        scratch_shapes=[
            pltpu.VMEM((hidden, width), half),
            pltpu.VMEM((hidden, width), half),
            pltpu.VMEM((4, 4, rows, width), half),
            pltpu.VMEM((3, 4, rows, width), jnp.float32),
            pltpu.VMEM((4, 4, rows, width), half),
            pltpu.VMEM((4, rows, ca), half),
            pltpu.VMEM((4, rows, ca), half),
            pltpu.VMEM((4, rows, cb), half),
            pltpu.VMEM((4, rows, cb), half),
            pltpu.VMEM((4, rows, ca), half),
            pltpu.VMEM((4, rows, cb), half),
            pltpu.VMEM((4, rows, width), half),
            pltpu.VMEM((4, rows, width), half),
            pltpu.VMEM((4, rows, ca), half),
            pltpu.VMEM((4, rows, cb), half),
            pltpu.SemaphoreType.DMA((2,)),
            pltpu.SemaphoreType.DMA((48,)),
            pltpu.SemaphoreType.DMA((5, 4)),
            pltpu.SemaphoreType.DMA((2,)),
            pltpu.SemaphoreType.DMA((5, 4)),
        ],
        cost_estimate=pl.CostEstimate(
            flops=4 * 16 * rows * width * hidden, bytes_accessed=4 * width * hidden, transcendentals=16 * rows * hidden
        ),
        compiler_params=pltpu.CompilerParams(
            collective_id=0, has_side_effects=True, vmem_limit_bytes=58 * 2**20
        ),
    )(normed, w_up.T, w_down)


EXTRA = ((16, 0, 5), (16, 1, 8), (17, 0, 6), (17, 1, 11), (18, 0, 4), (18, 1, 9))
PAIR = 2 * HEAD_DIM


def attend_kernel(
    rows, q_ref, k_ref, v_ref, text_ref, bias_ref, wo_ref, out_ref, st_ref, wo, land, kb, vb, res, att, wsem, ssem, xsem, rsem, osem, asem, lsem
):
    me = lax.axis_index("seq")
    mesh_id = pl.DeviceIdType.MESH
    deep = rows * 3 + 16

    def lanes(pair):
        return pl.ds(pl.multiple_of(pair * PAIR, PAIR), PAIR)

    def peer_of(k):
        return lax.rem(me + k, 16)

    def remote(src, dst, sent, got, peer):
        return pltpu.make_async_remote_copy(
            src_ref=src, dst_ref=dst, send_sem=sent, recv_sem=got, device_id={"seq": peer}, device_id_type=mesh_id
        )

    stack = [
        pltpu.make_async_copy(ref, st_ref.at[pl.ds(i * rows, ref.shape[0])], wsem.at[i + 1])
        for i, ref in enumerate((q_ref, k_ref, v_ref, text_ref))
    ]
    for copy in stack:
        copy.start()
    load = pltpu.make_async_copy(wo_ref, wo, wsem.at[0])
    load.start()
    own = pltpu.make_async_copy(st_ref.at[:, lanes(me)], land.at[0, me], lsem.at[0])
    barrier = pltpu.get_barrier_semaphore()

    def greet(k, c):
        pl.semaphore_signal(barrier, inc=1, device_id={"seq": peer_of(k)}, device_id_type=mesh_id)
        return c

    lax.fori_loop(1, 16, greet, 0)
    for copy in stack:
        copy.wait()
    own.start()
    pl.semaphore_wait(barrier, 15)

    def extra_in(e, pair, owner):
        return remote(st_ref.at[:, lanes(pair)], land.at[1, me], xsem.at[e], rsem.at[1, me], owner)

    def extra_own(pair):
        return pltpu.make_async_copy(st_ref.at[:, lanes(pair)], land.at[1, me], lsem.at[1])

    def pair_in(k):
        peer = peer_of(k)
        return remote(st_ref.at[:, lanes(peer)], land.at[0, me], ssem.at[k], rsem.at[0, me], peer)

    def go(k, c):
        pair_in(k).start()
        return c

    lax.fori_loop(1, 16, go, 0)
    for e, (pair, part, owner) in enumerate(EXTRA):

        @pl.when(me != owner)
        def _():
            extra_in(e, pair, owner).start()

        @pl.when(me == owner)
        def _():
            extra_own(pair).start()

    def back(u, dst, pair):
        return remote(res.at[u, dst], att.at[:, lanes(pair)], osem.at[u, dst], asem.at[pair], dst)

    def unit(u, pair, local, first, last):
        def arrive(k, c):
            src = peer_of(k)
            remote(land.at[u, src], land.at[u, src], ssem.at[0], rsem.at[u, src], src).wait_recv()
            return c

        lax.fori_loop(1, 16, arrive, 0)
        local.wait()
        text = land[u, :, 3 * rows : deep, :].reshape(256, PAIR)
        slot = lax.broadcasted_iota(jnp.int32, (64, 256), 0)
        place = lax.broadcasted_iota(jnp.int32, (64, 256), 1)
        start = (slot >> 2) * 16 + (slot & 3)
        for kind, buf in ((0, kb), (1, vb)):
            pick = jnp.where(place == start + 4 * kind, 1.0, 0.0).astype(jnp.bfloat16)
            buf[512:576, :] = jnp.dot(pick, text, preferred_element_type=jnp.float32).astype(jnp.bfloat16)
            buf[0:512, :] = land[u, :, (kind + 1) * rows : (kind + 2) * rows, :].reshape(512, PAIR)
        low = lax.broadcasted_iota(jnp.int32, (4 * rows, PAIR), 1) < HEAD_DIM

        def chunk(c, carry):
            made = []
            for part in range(2):
                q = land[u, pl.ds(c * 8 + part * 4, 4), 0:rows, :].reshape(4 * rows, PAIR)
                none = jnp.zeros_like(q)
                q_two = jnp.concatenate([jnp.where(low, q, none), jnp.where(low, none, q)], 0)
                scores = lax.dot_general(
                    q_two, kb[...], (((1,), (1,)), ((), ())), preferred_element_type=jnp.float32
                ) * (HEAD_DIM ** (-0.5))
                scores = scores + bias_ref[...]
                top = jnp.max(scores, -1, keepdims=True)
                weights = jnp.exp(scores - top)
                total = jnp.sum(weights, -1, keepdims=True)
                mixed = jnp.dot(weights.astype(jnp.bfloat16), vb[...], preferred_element_type=jnp.float32) / total
                made.append(jnp.where(low, mixed[: 4 * rows], mixed[4 * rows :]).astype(jnp.bfloat16))
            both = jnp.concatenate(made, 0)
            for j in range(8):
                dst = c * 8 + j
                res[u, dst] = both[j * rows : (j + 1) * rows, :]

                @pl.when(dst != me)
                def _():
                    back(u, dst, pair).start()

                @pl.when(dst == me)
                def _():
                    att[:, lanes(pair)] = both[j * rows : (j + 1) * rows, :]

            return carry

        lax.fori_loop(first, last, chunk, 0)

    unit(0, me, own, 0, 2)
    for e, (pair, part, owner) in enumerate(EXTRA):

        @pl.when(me == owner)
        def _():
            unit(1, pair, extra_own(pair), part, part + 1)

    def home(pair, src):
        spot = att.at[:, lanes(pair)]
        remote(spot, spot, ssem.at[0], asem.at[pair], src).wait_recv()

    def collect(k, c):
        home(peer_of(k), peer_of(k))
        return c

    lax.fori_loop(1, 16, collect, 0)
    for e, (pair, part, owner) in enumerate(EXTRA):

        @pl.when((me != owner) & (me // 8 == part))
        def _():
            home(pair, owner)

    load.wait()
    out_ref[...] = jnp.dot(att[...], wo[...], preferred_element_type=jnp.float32)

    def finish(k, c):
        pair_in(k).wait_send()
        back(0, peer_of(k), me).wait_send()
        return c

    lax.fori_loop(1, 16, finish, 0)
    for e, (pair, part, owner) in enumerate(EXTRA):

        @pl.when(me != owner)
        def _():
            extra_in(e, pair, owner).wait_send()

        @pl.when(me == owner)
        def _():
            def finish_extra(dst, c):
                @pl.when(dst != me)
                def _():
                    back(1, dst, pair).wait_send()

                return c

            lax.fori_loop(part * 8, part * 8 + 8, finish_extra, 0)


def attend_16(queries, image_keys, image_values, text_keys, text_values, w_out, length):
    rows, width = queries.shape
    half = jnp.bfloat16
    text = jnp.concatenate([text_keys, text_values, jnp.zeros((8, width), half)], 0)
    deep = 3 * rows + text.shape[0]
    key = jnp.arange(576, dtype=jnp.int32)
    bias = jnp.where(key - 512 < length, 0.0, -1e30).astype(jnp.float32)[None, :]
    pairs = width // PAIR
    return pl.pallas_call(
        functools.partial(attend_kernel, rows),
        out_shape=jax.ShapeDtypeStruct((rows, width), jnp.float32),
        in_specs=[
            pl.BlockSpec(memory_space=pl.ANY),
            pl.BlockSpec(memory_space=pl.ANY),
            pl.BlockSpec(memory_space=pl.ANY),
            pl.BlockSpec(memory_space=pl.ANY),
            pl.BlockSpec(memory_space=pltpu.VMEM),
            pl.BlockSpec(memory_space=pl.ANY),
        ],
        out_specs=pl.BlockSpec(memory_space=pltpu.VMEM),
        scratch_shapes=[
            pltpu.VMEM((deep, width), half),
            pltpu.VMEM((width, width), half),
            pltpu.VMEM((2, 16, deep, PAIR), half),
            pltpu.VMEM((576, PAIR), half),
            pltpu.VMEM((576, PAIR), half),
            pltpu.VMEM((2, 16, rows, PAIR), half),
            pltpu.VMEM((rows, width), half),
            pltpu.SemaphoreType.DMA((5,)),
            pltpu.SemaphoreType.DMA((16,)),
            pltpu.SemaphoreType.DMA((len(EXTRA),)),
            pltpu.SemaphoreType.DMA((2, 16)),
            pltpu.SemaphoreType.DMA((2, 16)),
            pltpu.SemaphoreType.DMA((pairs,)),
            pltpu.SemaphoreType.DMA((2,)),
        ],
        cost_estimate=pl.CostEstimate(
            flops=2 * rows * width * width, bytes_accessed=2 * width * width, transcendentals=2 * 512 * 576
        ),
        compiler_params=pltpu.CompilerParams(
            collective_id=1, has_side_effects=True, vmem_limit_bytes=58 * 2**20
        ),
    )(queries, image_keys, image_values, text, bias, w_out)


def ffn_any(normed, w_up, w_down):
    hidden_all = jax.nn.gelu(
        jnp.dot(
            lax.all_gather(normed, "seq", axis=0, tiled=True),
            w_up,
            preferred_element_type=jnp.float32,
        ),
        approximate=True,
    ).astype(jnp.bfloat16)
    mlp_out = lax.psum_scatter(
        jnp.dot(hidden_all, w_down, preferred_element_type=jnp.float32),
        "seq",
        scatter_dimension=0,
        tiled=True,
    )
    return mlp_out


def attend_any(queries, image_keys, image_values, text_keys, text_values, w_out, length):
    img_rows, width = queries.shape[1:]
    text_rows = text_keys.shape[1]
    both_rows = img_rows + text_rows
    score_scale = HEAD_DIM ** (-0.5)
    key_rows = jnp.concatenate([image_keys[0], text_keys[0]], 0)
    value_rows = jnp.concatenate([image_values[0], text_values[0]], 0)
    seq_count = lax.axis_size("seq")
    img_all = img_rows * seq_count
    unit_count = HEADS * img_rows
    head_span = min(HEADS, (unit_count - 1) // img_all + 2)
    slot_width = head_span * HEAD_DIM
    targets = jnp.arange(seq_count, dtype=jnp.int32)
    first_head = targets * unit_count // img_all
    slot_heads = first_head[:, None] + jnp.arange(head_span, dtype=jnp.int32)[None, :]

    def spread(rows):
        parts = []
        for target in range(seq_count):
            lead_head = target * unit_count // img_all
            for slot in range(lead_head, lead_head + head_span):
                head = min(slot, HEADS - 1)
                parts.append(rows[:, head * HEAD_DIM : (head + 1) * HEAD_DIM])
        return jnp.concatenate(parts, 1).reshape(rows.shape[0], seq_count, slot_width)

    query_in, key_in, value_in = (
        lax.all_to_all(spread(queries[0]), "seq", split_axis=1, concat_axis=1, tiled=True),
        lax.all_to_all(spread(key_rows), "seq", split_axis=1, concat_axis=1, tiled=True),
        lax.all_to_all(spread(value_rows), "seq", split_axis=1, concat_axis=1, tiled=True),
    )
    myself = lax.axis_index("seq")
    lead = myself * unit_count // img_all
    offset = myself * unit_count - lead * img_all
    query_flat = (
        query_in.reshape(img_rows, seq_count, head_span, HEAD_DIM)
        .transpose(2, 1, 0, 3)
        .reshape(head_span * img_all, HEAD_DIM)
    )
    query_units = lax.dynamic_slice_in_dim(query_flat, offset, unit_count, 0)
    unit_slot = (offset + jnp.arange(unit_count, dtype=jnp.int32)) // img_all
    slot_match = unit_slot[:, None] == jnp.arange(head_span, dtype=jnp.int32)[None, :]
    query_wide = jnp.where(
        slot_match[:, :, None], query_units[:, None, :], jnp.zeros((), jnp.bfloat16)
    ).reshape(unit_count, slot_width)
    key_count = both_rows * seq_count
    key_all = key_in.reshape(key_count, slot_width)
    value_all = value_in.reshape(key_count, slot_width)
    scores = (
        jnp.einsum("uw,kw->uk", query_wide, key_all, preferred_element_type=jnp.float32)
        * score_scale
    )
    local_row = jnp.arange(both_rows, dtype=jnp.int32)[:, None]
    text_slot = targets[None, :] * text_rows + local_row - img_rows
    valid = ((local_row < img_rows) | (text_slot < length)).reshape(-1)
    scores = jnp.where(valid[None, :], scores, -1e30)
    row_top = jnp.max(scores, -1, keepdims=True)
    weights = jnp.exp(scores - row_top)
    total = jnp.sum(weights, -1, keepdims=True)
    mixed = jnp.dot(
        weights.astype(jnp.bfloat16), value_all, preferred_element_type=jnp.float32
    ).reshape(unit_count, head_span, HEAD_DIM)
    picked = jnp.sum(jnp.where(slot_match[:, :, None], mixed, 0.0), 1)
    unit_out = (picked / total).astype(jnp.bfloat16)
    placed = lax.dynamic_update_slice_in_dim(
        jnp.zeros((head_span * img_all, HEAD_DIM), jnp.bfloat16), unit_out, offset, 0
    )
    going = (
        placed.reshape(head_span, seq_count, img_rows, HEAD_DIM)
        .transpose(2, 1, 0, 3)
        .reshape(img_rows, seq_count, slot_width)
    )
    coming = lax.all_to_all(going, "seq", split_axis=1, concat_axis=1, tiled=True)
    owner = (slot_heads[:, :, None] == jnp.arange(HEADS, dtype=jnp.int32)[None, None, :]).astype(
        jnp.bfloat16
    )
    attended = (
        jnp.einsum(
            "rjsd,jsh->rhd",
            coming.reshape(img_rows, seq_count, head_span, HEAD_DIM),
            owner,
            preferred_element_type=jnp.float32,
        )
        .reshape(img_rows, width)
        .astype(jnp.bfloat16)
    )
    return jnp.dot(attended, w_out, preferred_element_type=jnp.float32)


def body(
    queries,
    image_keys,
    image_values,
    text_keys,
    text_values,
    hidden_in,
    modulation,
    w_out,
    w_up,
    w_down,
    w_final,
    latent,
    text_len,
    step_index,
    guidance,
):
    img_rows = queries.shape[1]
    text_rows = text_keys.shape[1]
    width = queries.shape[2]
    length = text_len[0]
    seq_count = lax.axis_size("seq")
    if seq_count == 16 and (img_rows, text_rows, width) == (32, 4, 19 * PAIR):
        projected = attend_16(
            queries[0], image_keys[0], image_values[0], text_keys[0], text_values[0], w_out, length
        )
    else:
        projected = attend_any(queries, image_keys, image_values, text_keys, text_values, w_out, length)
    mods = modulation[0]
    middle = hidden_in[0].astype(jnp.float32) + mods[0] * projected
    normed = (layer_norm(middle) * (1.0 + mods[2]) + mods[1]).astype(jnp.bfloat16)
    if seq_count == 16 and img_rows == 32:
        mlp_out = ffn_16(normed, w_up, w_down)
    else:
        mlp_out = ffn_any(normed, w_up, w_down)
    final = middle + mods[3] * mlp_out
    head_in = (layer_norm(final) * (1.0 + mods[5]) + mods[4]).astype(jnp.bfloat16)
    own_velocity = jnp.dot(head_in, w_final, preferred_element_type=jnp.float32)
    step_size = sigma_at(step_index[0] + 1) - sigma_at(step_index[0])
    scale_now = guidance[0]
    half_width = latent.shape[1]
    partner = partner_2(own_velocity, "cfg", 0)
    is_cond = lax.axis_index("cfg") == 0
    cond_part = jnp.where(is_cond, own_velocity, partner)
    uncond_part = jnp.where(is_cond, partner, own_velocity)
    velocity_full = uncond_part + scale_now * (cond_part - uncond_part)
    velocity = lax.dynamic_slice_in_dim(
        velocity_full, lax.axis_index("cfg") * half_width, half_width, 1
    )
    next_latent = latent + step_size * velocity
    return (velocity, next_latent)


def solution(mesh):
    in_specs = (
        P("cfg", "seq", None),
        P("cfg", "seq", None),
        P("cfg", "seq", None),
        P("cfg", "seq", None),
        P("cfg", "seq", None),
        P("cfg", "seq", None),
        P("cfg", None, None),
        P(),
        P(None, "seq"),
        P("seq", None),
        P(),
        P("seq", "cfg"),
        P("cfg"),
        P(),
        P(),
    )
    out_specs = (P("seq", "cfg"), P("seq", "cfg"))
    return jax.shard_map(body, mesh=mesh, in_specs=in_specs, out_specs=out_specs, check_vma=False)
```

```python
import functools

import jax
import jax.numpy as jnp
from jax import lax
from jax.experimental import pallas as pl
from jax.experimental.pallas import tpu as pltpu
from jax.sharding import PartitionSpec as P

HEADS = 38
HEAD_DIM = 64
STEPS = 28


shift_value = 3.0
norm_eps = 1e-06


def partner_2(value, axis, bit):
    mask = 2**bit
    pairs = [(source, source ^ mask) for source in range(lax.axis_size(axis))]
    return lax.ppermute(value, axis, pairs)


def layer_norm(values):
    centred = values - jnp.mean(values, -1, keepdims=True)
    return centred / jnp.sqrt(jnp.mean(centred * centred, -1, keepdims=True) + norm_eps)


def sigma_at(index):
    frac = 1.0 - index.astype(jnp.float32) / STEPS
    return shift_value * frac / (1.0 + (shift_value - 1.0) * frac)


def ffn_kernel(
    ca, norm_ref, up_ref, down_ref, out_ref, wu, wd, g, pf, pb, ry0, ry1, rx0, rx1, rxa, ryb, rz, s0, s1, s2,
    wsem, ssem, gsem, dsem, esem
):
    me = lax.axis_index("seq")
    mz = me // 4
    mx = lax.rem(me, 2)
    my = lax.rem(me // 2, 2)
    xn = mz * 4 + my * 2 + (1 - mx)
    yn = mz * 4 + (1 - my) * 2 + mx
    zs = [mz, mz + 1 - 2 * lax.rem(mz, 2), lax.rem(mz + 2, 4), 3 - mz]
    zn = [z * 4 + my * 2 + mx for z in zs]
    width = norm_ref.shape[1]
    cols = (pl.ds(0, ca), pl.ds(ca, width - ca))
    a, b = cols
    load_up = pltpu.make_async_copy(up_ref, wu, wsem.at[0])
    load_down = pltpu.make_async_copy(down_ref, wd, wsem.at[1])
    load_up.start()
    load_down.start()
    barrier = pltpu.get_barrier_semaphore()
    peers = (xn, yn, zn[1], zn[2], zn[3])
    for peer in peers:
        pl.semaphore_signal(barrier, inc=1, device_id={"seq": peer}, device_id_type=pl.DeviceIdType.MESH)
    sent = []

    def send(src, dst, recv, peer):
        copy = pltpu.make_async_remote_copy(
            src_ref=src, dst_ref=dst, send_sem=ssem.at[len(sent)], recv_sem=recv,
            device_id={"seq": peer}, device_id_type=pl.DeviceIdType.MESH,
        )
        copy.start()
        sent.append(copy)

    def arrived(dst, recv):
        pltpu.make_async_remote_copy(
            src_ref=dst, dst_ref=dst, send_sem=ssem.at[0], recv_sem=recv,
            device_id={"seq": xn}, device_id_type=pl.DeviceIdType.MESH,
        ).wait_recv()

    g[0, mz] = norm_ref[...]
    pl.semaphore_wait(barrier, len(peers))
    for k in (1, 3, 2):
        send(norm_ref, g.at[0, mz], gsem.at[0, mz], zn[k])
    send(norm_ref, g.at[1, mz], gsem.at[1, mz], xn)
    send(norm_ref, g.at[2, mz], gsem.at[2, mz], yn)
    for k in (1, 3, 2):
        z = zs[k]
        arrived(g.at[0, z], gsem.at[0, z])
        send(g.at[0, z], g.at[1, z], gsem.at[1, z], xn)
        send(g.at[0, z], g.at[2, z], gsem.at[2, z], yn)

    def up(q):
        rows = g[q].reshape(128, width)
        wide = lax.dot_general(rows, wu[...], (((1,), (1,)), ((), ())), preferred_element_type=jnp.float32)
        return jax.nn.gelu(wide, approximate=True).astype(jnp.bfloat16)

    def down(hid, half):
        made = jnp.dot(hid, wd[:, cols[half]], preferred_element_type=jnp.float32)
        return made.reshape(4, 32, made.shape[1])

    load_up.wait()
    for k in (0, 1):
        z = zs[k]
        arrived(g.at[1, z], gsem.at[1, z])
        send(g.at[1, z, :, a], g.at[3, z, :, a], gsem.at[3, z], yn)
        arrived(g.at[2, z], gsem.at[2, z])
        send(g.at[2, z, :, b], g.at[3, z, :, b], gsem.at[4, z], xn)
    hid0 = up(0)
    for k in (3, 2):
        z = zs[k]
        arrived(g.at[1, z], gsem.at[1, z])
        send(g.at[1, z, :, a], g.at[3, z, :, a], gsem.at[3, z], yn)
        arrived(g.at[2, z], gsem.at[2, z])
        send(g.at[2, z, :, b], g.at[3, z, :, b], gsem.at[4, z], xn)
    load_down.wait()
    hid1 = up(1)
    pb[1, :, :, b] = down(hid1, 1).astype(jnp.bfloat16)
    send(pb.at[1, :, :, b], rx0, dsem.at[0], xn)
    hid2 = up(2)
    pb[2, :, :, a] = down(hid2, 0).astype(jnp.bfloat16)
    send(pb.at[2, :, :, a], ry0, dsem.at[1], yn)
    pf[1, :, :, a] = down(hid1, 0)
    pf[2, :, :, b] = down(hid2, 1)
    for z in zs:
        arrived(g.at[3, z, :, a], gsem.at[3, z])
        arrived(g.at[3, z, :, b], gsem.at[4, z])
    hid3 = up(3)
    order = (2, 1, 3, 0)
    pb[3, :, :, a] = down(hid3, 0).astype(jnp.bfloat16)
    for k in order:
        send(pb.at[3, zs[k], :, a], ry1.at[zs[k]], esem.at[0, zs[k]], yn)
    pb[3, :, :, b] = down(hid3, 1).astype(jnp.bfloat16)
    for k in order:
        send(pb.at[3, zs[k], :, b], rx1.at[zs[k]], esem.at[1, zs[k]], xn)
    pf[0, :, :, a] = down(hid0, 0)
    pf[0, :, :, b] = down(hid0, 1)
    for k in order:
        z = zs[k]
        arrived(ry1.at[z], esem.at[0, z])
        s1[z] = (pf[1, z, :, a] + ry1[z].astype(jnp.float32)).astype(jnp.bfloat16)
        send(s1.at[z], rxa.at[z], esem.at[2, z], xn)
        arrived(rx1.at[z], esem.at[1, z])
        s2[z] = (pf[2, z, :, b] + rx1[z].astype(jnp.float32)).astype(jnp.bfloat16)
        send(s2.at[z], ryb.at[z], esem.at[3, z], yn)
    arrived(rx0, dsem.at[0])
    arrived(ry0, dsem.at[1])
    for k in order:
        z = zs[k]
        arrived(rxa.at[z], esem.at[2, z])
        arrived(ryb.at[z], esem.at[3, z])
        sum_a = pf[0, z, :, a] + ry0[z].astype(jnp.float32) + rxa[z].astype(jnp.float32)
        sum_b = pf[0, z, :, b] + rx0[z].astype(jnp.float32) + ryb[z].astype(jnp.float32)
        if k:
            s0[z, :, a] = sum_a.astype(jnp.bfloat16)
            s0[z, :, b] = sum_b.astype(jnp.bfloat16)
            send(s0.at[z], rz.at[mz], esem.at[4, mz], zn[k])
        else:
            out_ref[:, a] = sum_a
            out_ref[:, b] = sum_b
    for k in (1, 3, 2):
        arrived(rz.at[zs[k]], esem.at[4, zs[k]])
        out_ref[...] += rz[zs[k]].astype(jnp.float32)
    for copy in sent:
        copy.wait_send()


def ffn_16(normed, w_up, w_down):
    rows, width = normed.shape
    hidden = w_up.shape[1]
    ca = (width // 128 + 1) // 2 * 128
    cb = width - ca
    half = jnp.bfloat16
    return pl.pallas_call(
        functools.partial(ffn_kernel, ca),
        out_shape=jax.ShapeDtypeStruct((rows, width), jnp.float32),
        in_specs=[
            pl.BlockSpec(memory_space=pltpu.VMEM),
            pl.BlockSpec(memory_space=pl.ANY),
            pl.BlockSpec(memory_space=pl.ANY),
        ],
        out_specs=pl.BlockSpec(memory_space=pltpu.VMEM),
        scratch_shapes=[
            pltpu.VMEM((hidden, width), half),
            pltpu.VMEM((hidden, width), half),
            pltpu.VMEM((4, 4, rows, width), half),
            pltpu.VMEM((3, 4, rows, width), jnp.float32),
            pltpu.VMEM((4, 4, rows, width), half),
            pltpu.VMEM((4, rows, ca), half),
            pltpu.VMEM((4, rows, ca), half),
            pltpu.VMEM((4, rows, cb), half),
            pltpu.VMEM((4, rows, cb), half),
            pltpu.VMEM((4, rows, ca), half),
            pltpu.VMEM((4, rows, cb), half),
            pltpu.VMEM((4, rows, width), half),
            pltpu.VMEM((4, rows, width), half),
            pltpu.VMEM((4, rows, ca), half),
            pltpu.VMEM((4, rows, cb), half),
            pltpu.SemaphoreType.DMA((2,)),
            pltpu.SemaphoreType.DMA((48,)),
            pltpu.SemaphoreType.DMA((5, 4)),
            pltpu.SemaphoreType.DMA((2,)),
            pltpu.SemaphoreType.DMA((5, 4)),
        ],
        cost_estimate=pl.CostEstimate(
            flops=4 * 16 * rows * width * hidden, bytes_accessed=4 * width * hidden, transcendentals=16 * rows * hidden
        ),
        compiler_params=pltpu.CompilerParams(
            collective_id=0, has_side_effects=True, vmem_limit_bytes=44 * 2**20
        ),
    )(normed, w_up.T, w_down)


EXTRA = ((16, 0, 5), (16, 1, 8), (17, 0, 6), (17, 1, 11), (18, 0, 4), (18, 1, 9))
PAIR = 2 * HEAD_DIM


def attend_kernel(
    rows, q_ref, k_ref, v_ref, text_ref, bias_ref, wo_ref, out_ref, st_ref, wo, land, kb, vb, res, att, wsem, ssem, xsem, rsem, osem, asem, lsem
):
    me = lax.axis_index("seq")
    mesh_id = pl.DeviceIdType.MESH
    deep = rows * 3 + 16

    def lanes(pair):
        return pl.ds(pl.multiple_of(pair * PAIR, PAIR), PAIR)

    def peer_of(k):
        return lax.rem(me + k, 16)

    def remote(src, dst, sent, got, peer):
        return pltpu.make_async_remote_copy(
            src_ref=src, dst_ref=dst, send_sem=sent, recv_sem=got, device_id={"seq": peer}, device_id_type=mesh_id
        )

    stack = [
        pltpu.make_async_copy(ref, st_ref.at[pl.ds(i * rows, ref.shape[0])], wsem.at[i + 1])
        for i, ref in enumerate((q_ref, k_ref, v_ref, text_ref))
    ]
    for copy in stack:
        copy.start()
    load = pltpu.make_async_copy(wo_ref, wo, wsem.at[0])
    load.start()
    own = pltpu.make_async_copy(st_ref.at[:, lanes(me)], land.at[0, me], lsem.at[0])
    barrier = pltpu.get_barrier_semaphore()

    def greet(k, c):
        pl.semaphore_signal(barrier, inc=1, device_id={"seq": peer_of(k)}, device_id_type=mesh_id)
        return c

    lax.fori_loop(1, 16, greet, 0)
    for copy in stack:
        copy.wait()
    own.start()
    pl.semaphore_wait(barrier, 15)

    def extra_in(e, pair, owner):
        return remote(st_ref.at[:, lanes(pair)], land.at[1, me], xsem.at[e], rsem.at[1, me], owner)

    def extra_own(pair):
        return pltpu.make_async_copy(st_ref.at[:, lanes(pair)], land.at[1, me], lsem.at[1])

    def pair_in(k):
        peer = peer_of(k)
        return remote(st_ref.at[:, lanes(peer)], land.at[0, me], ssem.at[k], rsem.at[0, me], peer)

    def go(k, c):
        pair_in(k).start()
        return c

    lax.fori_loop(1, 16, go, 0)
    for e, (pair, part, owner) in enumerate(EXTRA):

        @pl.when(me != owner)
        def _():
            extra_in(e, pair, owner).start()

        @pl.when(me == owner)
        def _():
            extra_own(pair).start()

    def back(u, dst, pair):
        return remote(res.at[u, dst], att.at[:, lanes(pair)], osem.at[u, dst], asem.at[pair], dst)

    def unit(u, pair, local, first, last):
        def arrive(k, c):
            src = peer_of(k)
            remote(land.at[u, src], land.at[u, src], ssem.at[0], rsem.at[u, src], src).wait_recv()
            return c

        lax.fori_loop(1, 16, arrive, 0)
        local.wait()
        text = land[u, :, 3 * rows : deep, :].reshape(256, PAIR)
        slot = lax.broadcasted_iota(jnp.int32, (64, 256), 0)
        place = lax.broadcasted_iota(jnp.int32, (64, 256), 1)
        start = (slot >> 2) * 16 + (slot & 3)
        for kind, buf in ((0, kb), (1, vb)):
            pick = jnp.where(place == start + 4 * kind, 1.0, 0.0).astype(jnp.bfloat16)
            buf[512:576, :] = jnp.dot(pick, text, preferred_element_type=jnp.float32).astype(jnp.bfloat16)
            buf[0:512, :] = land[u, :, (kind + 1) * rows : (kind + 2) * rows, :].reshape(512, PAIR)
        low = lax.broadcasted_iota(jnp.int32, (4 * rows, PAIR), 1) < HEAD_DIM

        def chunk(c, carry):
            made = []
            for part in range(2):
                q = land[u, pl.ds(c * 8 + part * 4, 4), 0:rows, :].reshape(4 * rows, PAIR)
                none = jnp.zeros_like(q)
                q_two = jnp.concatenate([jnp.where(low, q, none), jnp.where(low, none, q)], 0)
                scores = lax.dot_general(
                    q_two, kb[...], (((1,), (1,)), ((), ())), preferred_element_type=jnp.float32
                ) * (HEAD_DIM ** (-0.5))
                scores = scores + bias_ref[...]
                top = jnp.max(scores, -1, keepdims=True)
                weights = jnp.exp(scores - top)
                total = jnp.sum(weights, -1, keepdims=True)
                mixed = jnp.dot(weights.astype(jnp.bfloat16), vb[...], preferred_element_type=jnp.float32) / total
                made.append(jnp.where(low, mixed[: 4 * rows], mixed[4 * rows :]).astype(jnp.bfloat16))
            both = jnp.concatenate(made, 0)
            for j in range(8):
                dst = c * 8 + j
                res[u, dst] = both[j * rows : (j + 1) * rows, :]

                @pl.when(dst != me)
                def _():
                    back(u, dst, pair).start()

                @pl.when(dst == me)
                def _():
                    att[:, lanes(pair)] = both[j * rows : (j + 1) * rows, :]

            return carry

        lax.fori_loop(first, last, chunk, 0)

    unit(0, me, own, 0, 2)
    for e, (pair, part, owner) in enumerate(EXTRA):

        @pl.when(me == owner)
        def _():
            unit(1, pair, extra_own(pair), part, part + 1)

    def home(pair, src):
        spot = att.at[:, lanes(pair)]
        remote(spot, spot, ssem.at[0], asem.at[pair], src).wait_recv()

    def collect(k, c):
        home(peer_of(k), peer_of(k))
        return c

    lax.fori_loop(1, 16, collect, 0)
    for e, (pair, part, owner) in enumerate(EXTRA):

        @pl.when((me != owner) & (me // 8 == part))
        def _():
            home(pair, owner)

    load.wait()
    out_ref[...] = jnp.dot(att[...], wo[...], preferred_element_type=jnp.float32)

    def finish(k, c):
        pair_in(k).wait_send()
        back(0, peer_of(k), me).wait_send()
        return c

    lax.fori_loop(1, 16, finish, 0)
    for e, (pair, part, owner) in enumerate(EXTRA):

        @pl.when(me != owner)
        def _():
            extra_in(e, pair, owner).wait_send()

        @pl.when(me == owner)
        def _():
            def finish_extra(dst, c):
                @pl.when(dst != me)
                def _():
                    back(1, dst, pair).wait_send()

                return c

            lax.fori_loop(part * 8, part * 8 + 8, finish_extra, 0)


def attend_16(queries, image_keys, image_values, text_keys, text_values, w_out, length):
    rows, width = queries.shape
    half = jnp.bfloat16
    text = jnp.concatenate([text_keys, text_values, jnp.zeros((8, width), half)], 0)
    deep = 3 * rows + text.shape[0]
    key = jnp.arange(576, dtype=jnp.int32)
    bias = jnp.where(key - 512 < length, 0.0, -1e30).astype(jnp.float32)[None, :]
    pairs = width // PAIR
    return pl.pallas_call(
        functools.partial(attend_kernel, rows),
        out_shape=jax.ShapeDtypeStruct((rows, width), jnp.float32),
        in_specs=[
            pl.BlockSpec(memory_space=pl.ANY),
            pl.BlockSpec(memory_space=pl.ANY),
            pl.BlockSpec(memory_space=pl.ANY),
            pl.BlockSpec(memory_space=pl.ANY),
            pl.BlockSpec(memory_space=pltpu.VMEM),
            pl.BlockSpec(memory_space=pl.ANY),
        ],
        out_specs=pl.BlockSpec(memory_space=pltpu.VMEM),
        scratch_shapes=[
            pltpu.VMEM((deep, width), half),
            pltpu.VMEM((width, width), half),
            pltpu.VMEM((2, 16, deep, PAIR), half),
            pltpu.VMEM((576, PAIR), half),
            pltpu.VMEM((576, PAIR), half),
            pltpu.VMEM((2, 16, rows, PAIR), half),
            pltpu.VMEM((rows, width), half),
            pltpu.SemaphoreType.DMA((5,)),
            pltpu.SemaphoreType.DMA((16,)),
            pltpu.SemaphoreType.DMA((len(EXTRA),)),
            pltpu.SemaphoreType.DMA((2, 16)),
            pltpu.SemaphoreType.DMA((2, 16)),
            pltpu.SemaphoreType.DMA((pairs,)),
            pltpu.SemaphoreType.DMA((2,)),
        ],
        cost_estimate=pl.CostEstimate(
            flops=2 * rows * width * width, bytes_accessed=2 * width * width, transcendentals=2 * 512 * 576
        ),
        compiler_params=pltpu.CompilerParams(
            collective_id=1, has_side_effects=True, vmem_limit_bytes=44 * 2**20
        ),
    )(queries, image_keys, image_values, text, bias, w_out)


def ffn_any(normed, w_up, w_down):
    hidden_all = jax.nn.gelu(
        jnp.dot(
            lax.all_gather(normed, "seq", axis=0, tiled=True),
            w_up,
            preferred_element_type=jnp.float32,
        ),
        approximate=True,
    ).astype(jnp.bfloat16)
    mlp_out = lax.psum_scatter(
        jnp.dot(hidden_all, w_down, preferred_element_type=jnp.float32),
        "seq",
        scatter_dimension=0,
        tiled=True,
    )
    return mlp_out


def attend_any(queries, image_keys, image_values, text_keys, text_values, w_out, length):
    img_rows, width = queries.shape[1:]
    text_rows = text_keys.shape[1]
    both_rows = img_rows + text_rows
    score_scale = HEAD_DIM ** (-0.5)
    key_rows = jnp.concatenate([image_keys[0], text_keys[0]], 0)
    value_rows = jnp.concatenate([image_values[0], text_values[0]], 0)
    seq_count = lax.axis_size("seq")
    img_all = img_rows * seq_count
    unit_count = HEADS * img_rows
    head_span = min(HEADS, (unit_count - 1) // img_all + 2)
    slot_width = head_span * HEAD_DIM
    targets = jnp.arange(seq_count, dtype=jnp.int32)
    first_head = targets * unit_count // img_all
    slot_heads = first_head[:, None] + jnp.arange(head_span, dtype=jnp.int32)[None, :]

    def spread(rows):
        parts = []
        for target in range(seq_count):
            lead_head = target * unit_count // img_all
            for slot in range(lead_head, lead_head + head_span):
                head = min(slot, HEADS - 1)
                parts.append(rows[:, head * HEAD_DIM : (head + 1) * HEAD_DIM])
        return jnp.concatenate(parts, 1).reshape(rows.shape[0], seq_count, slot_width)

    query_in, key_in, value_in = (
        lax.all_to_all(spread(queries[0]), "seq", split_axis=1, concat_axis=1, tiled=True),
        lax.all_to_all(spread(key_rows), "seq", split_axis=1, concat_axis=1, tiled=True),
        lax.all_to_all(spread(value_rows), "seq", split_axis=1, concat_axis=1, tiled=True),
    )
    myself = lax.axis_index("seq")
    lead = myself * unit_count // img_all
    offset = myself * unit_count - lead * img_all
    query_flat = (
        query_in.reshape(img_rows, seq_count, head_span, HEAD_DIM)
        .transpose(2, 1, 0, 3)
        .reshape(head_span * img_all, HEAD_DIM)
    )
    query_units = lax.dynamic_slice_in_dim(query_flat, offset, unit_count, 0)
    unit_slot = (offset + jnp.arange(unit_count, dtype=jnp.int32)) // img_all
    slot_match = unit_slot[:, None] == jnp.arange(head_span, dtype=jnp.int32)[None, :]
    query_wide = jnp.where(
        slot_match[:, :, None], query_units[:, None, :], jnp.zeros((), jnp.bfloat16)
    ).reshape(unit_count, slot_width)
    key_count = both_rows * seq_count
    key_all = key_in.reshape(key_count, slot_width)
    value_all = value_in.reshape(key_count, slot_width)
    scores = (
        jnp.einsum("uw,kw->uk", query_wide, key_all, preferred_element_type=jnp.float32)
        * score_scale
    )
    local_row = jnp.arange(both_rows, dtype=jnp.int32)[:, None]
    text_slot = targets[None, :] * text_rows + local_row - img_rows
    valid = ((local_row < img_rows) | (text_slot < length)).reshape(-1)
    scores = jnp.where(valid[None, :], scores, -1e30)
    row_top = jnp.max(scores, -1, keepdims=True)
    weights = jnp.exp(scores - row_top)
    total = jnp.sum(weights, -1, keepdims=True)
    mixed = jnp.dot(
        weights.astype(jnp.bfloat16), value_all, preferred_element_type=jnp.float32
    ).reshape(unit_count, head_span, HEAD_DIM)
    picked = jnp.sum(jnp.where(slot_match[:, :, None], mixed, 0.0), 1)
    unit_out = (picked / total).astype(jnp.bfloat16)
    placed = lax.dynamic_update_slice_in_dim(
        jnp.zeros((head_span * img_all, HEAD_DIM), jnp.bfloat16), unit_out, offset, 0
    )
    going = (
        placed.reshape(head_span, seq_count, img_rows, HEAD_DIM)
        .transpose(2, 1, 0, 3)
        .reshape(img_rows, seq_count, slot_width)
    )
    coming = lax.all_to_all(going, "seq", split_axis=1, concat_axis=1, tiled=True)
    owner = (slot_heads[:, :, None] == jnp.arange(HEADS, dtype=jnp.int32)[None, None, :]).astype(
        jnp.bfloat16
    )
    attended = (
        jnp.einsum(
            "rjsd,jsh->rhd",
            coming.reshape(img_rows, seq_count, head_span, HEAD_DIM),
            owner,
            preferred_element_type=jnp.float32,
        )
        .reshape(img_rows, width)
        .astype(jnp.bfloat16)
    )
    return jnp.dot(attended, w_out, preferred_element_type=jnp.float32)


def body(
    queries,
    image_keys,
    image_values,
    text_keys,
    text_values,
    hidden_in,
    modulation,
    w_out,
    w_up,
    w_down,
    w_final,
    latent,
    text_len,
    step_index,
    guidance,
):
    img_rows = queries.shape[1]
    text_rows = text_keys.shape[1]
    width = queries.shape[2]
    length = text_len[0]
    seq_count = lax.axis_size("seq")
    if seq_count == 16 and (img_rows, text_rows, width) == (32, 4, 19 * PAIR):
        projected = attend_16(
            queries[0], image_keys[0], image_values[0], text_keys[0], text_values[0], w_out, length
        )
    else:
        projected = attend_any(queries, image_keys, image_values, text_keys, text_values, w_out, length)
    mods = modulation[0]
    middle = hidden_in[0].astype(jnp.float32) + mods[0] * projected
    normed = (layer_norm(middle) * (1.0 + mods[2]) + mods[1]).astype(jnp.bfloat16)
    if seq_count == 16 and img_rows == 32:
        mlp_out = ffn_16(normed, w_up, w_down)
    else:
        mlp_out = ffn_any(normed, w_up, w_down)
    final = middle + mods[3] * mlp_out
    head_in = (layer_norm(final) * (1.0 + mods[5]) + mods[4]).astype(jnp.bfloat16)
    own_velocity = jnp.dot(head_in, w_final, preferred_element_type=jnp.float32)
    step_size = sigma_at(step_index[0] + 1) - sigma_at(step_index[0])
    scale_now = guidance[0]
    half_width = latent.shape[1]
    partner = partner_2(own_velocity, "cfg", 0)
    is_cond = lax.axis_index("cfg") == 0
    cond_part = jnp.where(is_cond, own_velocity, partner)
    uncond_part = jnp.where(is_cond, partner, own_velocity)
    velocity_full = uncond_part + scale_now * (cond_part - uncond_part)
    velocity = lax.dynamic_slice_in_dim(
        velocity_full, lax.axis_index("cfg") * half_width, half_width, 1
    )
    next_latent = latent + step_size * velocity
    return (velocity, next_latent)


def solution(mesh):
    in_specs = (
        P("cfg", "seq", None),
        P("cfg", "seq", None),
        P("cfg", "seq", None),
        P("cfg", "seq", None),
        P("cfg", "seq", None),
        P("cfg", "seq", None),
        P("cfg", None, None),
        P(),
        P(None, "seq"),
        P("seq", None),
        P(),
        P("seq", "cfg"),
        P("cfg"),
        P(),
        P(),
    )
    out_specs = (P("seq", "cfg"), P("seq", "cfg"))
    return jax.shard_map(body, mesh=mesh, in_specs=in_specs, out_specs=out_specs, check_vma=False)
```
